32 devices in a mesh: groups: 2 (over y), space: 16 (over z, x, core).
Axes of the slice: x: 2, y: 2, z: 4, core: 2. Of those that a mesh axis runs over, the one named last changes fastest.
Arguments:
- latent: bfloat16 [2048, 8, 1024], P(('groups', 'space')), parts along dimension 0, may hold values from -6 to 6
- w_src: bfloat16 [1024, 1024], replicated, may hold values from -0.1875 to 0.1875
- b_hidden: float32 [1024], replicated, may hold values from -3 to 3
- w_out: bfloat16 [1024, 100], replicated, may hold values from -0.1875 to 0.1875
- b_out: float32 [100], replicated, may hold values from -3 to 3
- targets: float32 [100, 8192], P(None, ('groups', 'space')), parts along dimension 1, may hold values from -6 to 6
- var_weight: float32 [100], replicated, may hold values from 0.2 to 2
- area_weight: float32 [4096], P('space'), may hold values from 0.5 to 18
- edge_src: int32 [4096, 3], P('space'), may hold values from 0 to 95, as said below
- edge_coef: float32 [4096, 3], P('space'), may hold values from 0.2 to 1
- send_rows: int32 [16, 16, 2], P('space'), may hold values from -1 to 63, as said below
Outputs:
- loss: float32 [2], P('groups'), parts along dimension 0
- grad_latent: float32 [2048, 8, 1024], P(('groups', 'space')), parts along dimension 0
- grad_w_src: float32 [2048, 1024], P(('groups', 'space')), parts along dimension 0
- grad_w_out: float32 [2048, 100], P(('groups', 'space')), parts along dimension 0
The draws below stay inside these ranges and needn't reach their ends.
There are 2 independent parts, one for each index of `groups`. The reference program is written for one: setup_inputs(seed, part) draws one part's arguments, and reference() takes and returns one part's arrays. A program takes and returns all parts, laid end to end along the dimension named above; an argument that names none is the same for every part. Nothing has to cross between parts.
Inputs may be any that keep to these rules, and one draw needn't show every extreme that they name: `send_rows`: -1 marks an empty slot, other entries are rows of the sender's 64 mesh nodes; filled slots come first; every sender fills at least one slot for every receiver, and some receiver gets all 2 slots filled by every sender. `edge_src`: an entry below 64 is a mesh row of the grid point's own device; an entry 64 + s * 2 + b names a filled slot b of sender s for that device.
All inputs are finite; a program needn't handle non-finite values.
Results may differ from the reference program's by a relative error of at most 0.013.
Values may be sent and summed in bfloat16 or wider, within the bound.
No kernel may reach another device: no remote copies, remote signals or barrier semaphores. Data moves between devices by JAX's collectives and lax.ppermute only.
A program may use at most 128 MiB of HBM per device.

```python
import math
from functools import reduce
import jax
import jax.numpy as jnp
from jax import lax

H = 1024
V = 100
M = 8
K = 3
SLOTS = 2
WSCALE = 2048
G_DEV = 256
MESH_DEV = 64
GRID = 4096
MESH = 1024
N_SPACE = 16


def pair_counts(key):
    base = jax.random.randint(jax.random.fold_in(key, 101), (N_SPACE, N_SPACE), 1, SLOTS + 1)
    full_receiver = jax.random.randint(jax.random.fold_in(key, 102), (), 0, N_SPACE)
    sender = jnp.arange(N_SPACE)[:, None]
    receiver = jnp.arange(N_SPACE)[None, :]
    forced = (receiver == full_receiver) | (sender == N_SPACE - 1) | ((sender + receiver) % 5 == 0)
    return jnp.where(forced, SLOTS, base).astype(jnp.int32)


def draw_send_rows(key, part):
    counts = pair_counts(key)
    key = jax.random.fold_in(key, 1)
    picked = jax.random.randint(key, (N_SPACE, N_SPACE, SLOTS), 0, MESH_DEV)
    slot_index = jnp.arange(SLOTS)[None, None, :]
    diagonal = jnp.eye(N_SPACE, dtype=jnp.int32)[:, :, None] > 0
    picked = jnp.where(diagonal & (slot_index == 0), MESH_DEV - 1, picked)
    live = slot_index < counts[:, :, None]
    return jnp.where(live, picked, -1).astype(jnp.int32)


def draw_edge_src(key, part):
    counts = pair_counts(key)
    key = jax.random.fold_in(key, 2)
    key_local, key_row, key_sender, key_slot = jax.random.split(key, 4)
    shape = (N_SPACE, G_DEV, K)
    receiver = jnp.broadcast_to(jnp.arange(N_SPACE)[:, None, None], shape)
    local_pick = jax.random.randint(key_local, shape, 0, 4) == 0
    local_row = jax.random.randint(key_row, shape, 0, MESH_DEV)
    sender = jax.random.randint(key_sender, shape, 0, N_SPACE)
    available = counts[sender, receiver]
    slot_pick = jax.random.randint(key_slot, shape, 0, 1 << 20) % available
    remote = MESH_DEV + sender * SLOTS + slot_pick
    chosen = jnp.where(local_pick, local_row, remote)
    chosen = chosen.at[:, 0, 0].set(MESH_DEV + N_SPACE * SLOTS - 1)
    return chosen.reshape(GRID, K).astype(jnp.int32)


def draw_area_weight(key, part):
    key = jax.random.fold_in(key, 3)
    base = jax.random.uniform(key, (N_SPACE, G_DEV), jnp.float32, 0.5, 2.0)
    ramp = 1.0 + 2.0 * jnp.arange(N_SPACE, dtype=jnp.float32) / max(N_SPACE - 1, 1)
    return (base * ramp[:, None]).reshape(GRID).astype(jnp.float32)


def level_of(own_key, extent, cuts, low, high):
    loudness, own = 1.0, jax.random.fold_in(own_key, 6)
    for dim, parts in cuts:
        draws = jnp.exp(jax.random.uniform(jax.random.fold_in(own, dim), (parts,), jnp.float32, low / len(cuts), high / len(cuts)))
        loudness = loudness * jnp.repeat(draws, extent[dim] // parts).reshape([-1 if axis == dim else 1 for axis in range(len(extent))])
    return loudness


def centred(stream_key, shape, deviation, most, cuts=(), kind=jnp.bfloat16):
    gain = level_of(stream_key, shape, cuts, -0.22, 0.18) if cuts else 1.0
    drawn = jax.random.normal(stream_key, shape, jnp.float32) * deviation * gain
    return jnp.minimum(jnp.maximum(drawn, -most), most).astype(kind)


def setup_inputs(seed: int = 0, part: int = 0) -> dict:
    keys = jax.random.split(jax.random.key(seed), 12)
    part_splits = jax.random.split(jax.random.fold_in(keys[11], part), 12)
    latent = centred(part_splits[0], (MESH, M, H), 1.0, 6.0, ((0, 16),))
    w_src = centred(keys[1], (H, H), H ** -0.5, 0.1875)
    b_hidden = centred(keys[2], (H,), 0.5, 3.0, (), jnp.float32)
    w_out = centred(keys[3], (H, V), H ** -0.5, 0.1875)
    b_out = centred(keys[4], (V,), 0.5, 3.0, (), jnp.float32)
    targets = centred(part_splits[5], (V, GRID), 1.0, 6.0, ((1, 16),), jnp.float32)
    var_weight = jnp.clip(jnp.exp(jax.random.uniform(keys[6], (V,), jnp.float32, math.log(0.2), math.log(2.0))), 0.2, 2.0)
    area_weight = draw_area_weight(jax.random.fold_in(keys[11], 71), part)
    edge_src = draw_edge_src(jax.random.fold_in(keys[11], 71), part)
    edge_coef = jnp.clip(0.2 + 0.8 * jax.random.uniform(keys[9], (GRID, K), jnp.float32) ** level_of(keys[9], (GRID, K), ((0, 16),), -0.2, 0.2), 0.2, 1.0)
    send_rows = draw_send_rows(jax.random.fold_in(keys[11], 71), part)
    return dict(latent=latent, w_src=w_src, b_hidden=b_hidden, w_out=w_out, b_out=b_out, targets=targets, var_weight=var_weight, area_weight=area_weight, edge_src=edge_src, edge_coef=edge_coef, send_rows=send_rows)


alpha_fair = 0.95
smooth_sq = 0.01

def spread_coef(members):
    return alpha_fair / (2.0 * members * (members - 1)) + (1.0 - alpha_fair) / (2.0 * members * members)

def shard_work(lookup, edge_src, edge_coef, targets, area_weight, var_weight, b_hidden, w_out, b_out, mean_area):
    grid_dev = targets.shape[1]
    block_size = 128 if grid_dev % 128 == 0 else grid_dev
    members = lookup.shape[1]
    spread = spread_coef(members)
    offdiag = 1.0 - jnp.eye(members, dtype=jnp.float32)
    w_float = w_out.astype(jnp.float32)

    def one_block(carry, index):
        loss_sum, dwout, dtable = carry
        first = index * block_size
        source_idx = lax.dynamic_slice_in_dim(edge_src, first, block_size, 0)
        edge_weight = lax.dynamic_slice_in_dim(edge_coef, first, block_size, 0)
        truth = lax.dynamic_slice_in_dim(targets, first, block_size, 1)
        block_area = lax.dynamic_slice_in_dim(area_weight, first, block_size, 0)
        terms = [edge_weight[:, j, None, None] * lookup[source_idx[:, j]].astype(jnp.float32) for j in range(source_idx.shape[1])]
        preact = reduce(jnp.add, terms) + b_hidden
        hidden, gelu_back = jax.vjp(jax.nn.gelu, preact)
        hidden_b = hidden.astype(jnp.bfloat16)
        pred = jnp.einsum('gmh,hv->mvg', hidden_b.astype(jnp.float32), w_float) + b_out[None, :, None]
        misfit = pred - truth[None]
        smooth = jnp.sqrt(misfit * misfit + smooth_sq)
        pairwise = pred[:, None] - pred[None, :]
        pair_smooth = jnp.sqrt(pairwise * pairwise + smooth_sq)
        crps_score = lax.optimization_barrier(jnp.mean(smooth, axis=0)) - spread * lax.optimization_barrier(jnp.sum(pair_smooth * offdiag[:, :, None, None], axis=(0, 1)))
        weighting = var_weight[:, None] * block_area[None, :]
        loss_sum = loss_sum + jnp.sum(weighting * crps_score)
        gradient = misfit / smooth / members - 2.0 * spread * lax.optimization_barrier(jnp.sum(pairwise / pair_smooth * offdiag[:, :, None, None], axis=1))
        dpred = (gradient * (weighting / mean_area)[None]).astype(jnp.bfloat16)
        dpred_f = dpred.astype(jnp.float32)
        dhidden = jnp.einsum('mvg,hv->gmh', dpred_f, w_float)
        dpreact = gelu_back(dhidden)[0].astype(jnp.bfloat16).astype(jnp.float32)
        dwout = dwout + jnp.einsum('gmh,mvg->hv', hidden_b.astype(jnp.float32), dpred_f)
        for j in range(source_idx.shape[1]):
            dtable = dtable.at[source_idx[:, j]].add(edge_weight[:, j, None, None] * dpreact)
        return ((loss_sum, dwout, dtable), None)
    init = (jnp.zeros((), jnp.float32), jnp.zeros(w_out.shape, jnp.float32), jnp.zeros(lookup.shape, jnp.float32))
    result, _ = lax.scan(one_block, init, jnp.arange(grid_dev // block_size, dtype=jnp.int32))
    return result

def reference(latent, w_src, b_hidden, w_out, b_out, targets, var_weight, area_weight, edge_src, edge_coef, send_rows):
    latent_flat = latent.reshape(MESH * M, H)
    projected = jnp.dot(latent_flat, w_src, preferred_element_type=jnp.float32).astype(jnp.bfloat16).reshape(MESH, M, H)
    mean_area = jnp.sum(area_weight) / GRID
    owner = jnp.arange(N_SPACE, dtype=jnp.int32)[:, None]

    def shard_step(carry, shard):
        loss_sum, dwout, dproj = carry
        slot_rows = send_rows[:, shard, :]
        global_row = owner * MESH_DEV + jnp.maximum(slot_rows, 0)
        incoming = jnp.where((slot_rows >= 0)[:, :, None, None], projected[global_row], jnp.zeros((), jnp.bfloat16))
        own_rows = lax.dynamic_slice_in_dim(projected, (shard * MESH_DEV).astype(jnp.int32), MESH_DEV, 0)
        lookup = jnp.concatenate([own_rows, incoming.reshape(N_SPACE * SLOTS, M, H)], axis=0)
        grid_first = (shard * G_DEV).astype(jnp.int32)
        part_loss, part_dwout, dtable = shard_work(lookup, lax.dynamic_slice_in_dim(edge_src, grid_first, G_DEV, 0), lax.dynamic_slice_in_dim(edge_coef, grid_first, G_DEV, 0), lax.dynamic_slice_in_dim(targets, grid_first, G_DEV, 1), lax.dynamic_slice_in_dim(area_weight, grid_first, G_DEV, 0), var_weight, b_hidden, w_out, b_out, mean_area)
        mesh_first = (shard * MESH_DEV).astype(jnp.int32)
        current = lax.dynamic_slice_in_dim(dproj, mesh_first, MESH_DEV, 0)
        dproj = lax.dynamic_update_slice_in_dim(dproj, current + dtable[:MESH_DEV], mesh_first, 0)
        slot_grad = lax.optimization_barrier(dtable[MESH_DEV:].astype(jnp.bfloat16)).astype(jnp.float32)
        destination = jnp.where(slot_rows >= 0, global_row, MESH).reshape(N_SPACE * SLOTS)
        dproj = dproj.at[destination].add(slot_grad)
        return ((loss_sum + part_loss, dwout + part_dwout, dproj), None)
    init = (jnp.zeros((), jnp.float32), jnp.zeros((H, V), jnp.float32), jnp.zeros((MESH + 1, M, H), jnp.float32))
    (loss_sum, dwout, dproj), _ = lax.scan(shard_step, init, jnp.arange(N_SPACE, dtype=jnp.int32))
    dprojected = dproj[:MESH].astype(jnp.bfloat16).reshape(MESH * M, H)
    grad_latent = jnp.dot(dprojected, w_src.T, preferred_element_type=jnp.float32).reshape(MESH, M, H)
    grad_scale = WSCALE / GRID
    grad_w_src = jnp.dot(latent_flat.T, dprojected, preferred_element_type=jnp.float32) * grad_scale
    grad_w_out = dwout * grad_scale
    loss = jnp.reshape(loss_sum / (mean_area * GRID), (1,))
    return (loss, grad_latent, grad_w_src, grad_w_out)
```

```python
import functools
import math

import jax
import jax.numpy as jnp
from jax import lax
from jax.experimental import pallas as pl
from jax.experimental.pallas import tpu as pltpu
from jax.sharding import PartitionSpec as P

WSCALE = 2048
LANES = 128
ROWS = 16
alpha_fair = 0.95
smooth_sq = 0.01
VMEM_BYTES = 56 * 1024 * 1024

f32 = jnp.float32
bf16 = jnp.bfloat16
TN = (((0,), (0,)), ((), ()))
NT = (((1,), (1,)), ((), ()))
SMEM = pl.BlockSpec(memory_space=pltpu.SMEM)
VMEM = pl.BlockSpec(memory_space=pltpu.VMEM)


def spread_coef(members):
    return alpha_fair / (2.0 * members * (members - 1)) + (1.0 - alpha_fair) / (
        2.0 * members * members
    )


def mm(a, b, dims=(((1,), (0,)), ((), ()))):
    return lax.dot_general(a, b, dims, preferred_element_type=f32)


def round_up(value, multiple):
    return -(-value // multiple) * multiple


def split_sum(value):
    high = value.astype(bf16)
    rest = value - high.astype(f32)
    middle = rest.astype(bf16)
    return high, middle, (rest - middle.astype(f32)).astype(bf16)


def fill_selector(rows_ref, selector, shards, slots, members):
    lane = lax.broadcasted_iota(jnp.int32, (members, selector.shape[1]), 1)
    member = lax.broadcasted_iota(jnp.int32, (members, selector.shape[1]), 0)
    for s in range(shards):
        for b in range(slots):
            row = rows_ref[0, b, s]
            first = (s * slots + b) * members
            selector[first : first + members, :] = jnp.where(
                lane == row * members + member, 1.0, 0.0
            ).astype(f32)


def project(projected, rows, w_src):
    out = mm(rows, w_src[...])
    for c in range(projected.shape[0]):
        projected[c, : rows.shape[0], :] = out[:, c * LANES : (c + 1) * LANES]


def by_member(projected, table, first, count):
    members = table.shape[0]
    for m in range(members):
        for c in range(projected.shape[0]):
            block = projected[c, pl.ds(m, count, stride=members), :]
            table[m, first : first + count, c * LANES : (c + 1) * LANES] = block.astype(bf16)


def pack_kernel(rows_ref, latent, area, out, selector, *, members, slots):
    shards, per_pair, _ = out.shape
    width = latent.shape[1]
    fill_selector(rows_ref, selector, shards, slots, members)
    picked = mm(selector[...].astype(bf16), latent[...])
    out[:, :, :width] = picked.astype(bf16).reshape(shards, per_pair, width)
    total = jnp.sum(area[...], axis=1, keepdims=True) + jnp.zeros((per_pair, LANES), f32)
    lane = lax.broadcasted_iota(jnp.int32, (per_pair, LANES), 1)
    tail = jnp.zeros((per_pair, LANES), f32)
    for i, piece in enumerate(split_sum(total)):
        tail = jnp.where(lane == i, piece.astype(f32), tail)
    tail = tail.astype(bf16)
    for s in range(shards):
        out[s, :, width:] = tail


def local_kernel(
    latent, w_src, edge_src, edge_coef, table, edge_gr, edge_rg, projected, *, members
):
    mesh_rows = table.shape[1]
    project(projected, latent[...], w_src)
    by_member(projected, table, 0, mesh_rows)
    rows, points = edge_rg.shape
    row = lax.broadcasted_iota(jnp.int32, (rows, points), 0)
    matrix = jnp.zeros((rows, points), f32)
    for k in range(edge_src.shape[0]):
        matrix = matrix + jnp.where(
            row == edge_src[k : k + 1, :], edge_coef[k : k + 1, :], 0.0
        )
    edge_rg[...] = matrix.astype(bf16)
    edge_gr[...] = matrix.T.astype(bf16)


def decoder_kernel(
    me_ref,
    arrived,
    local,
    latent,
    w_src,
    edge_gr,
    edge_rg,
    b_hidden,
    w_out_t,
    b_out,
    targets,
    var_weight,
    area_weight,
    dlocal,
    slot_grad,
    keep_a,
    send_a,
    keep_b,
    send_b,
    table,
    hidden,
    slope,
    preact,
    pred,
    dpred,
    dtable,
    dtable_low,
    partial,
    *,
    points_all,
    variables,
):
    members, mesh_rows, width = local.shape
    shards, per_pair, _ = arrived.shape
    received = shards * per_pair
    rows, points = edge_rg.shape
    var_pad = w_out_t.shape[0]
    var_rows = round_up(variables, ROWS)
    me = me_ref[0]

    arrived_rows = arrived[:, :, :width].reshape(received, width)
    project(dtable, arrived_rows, w_src)
    table[:, :mesh_rows, :] = local[...]
    by_member(dtable, table, mesh_rows, received // members)

    tail = arrived[:, :, width:].astype(f32)
    at_row = lax.broadcasted_iota(jnp.int32, tail.shape, 1)
    at_lane = lax.broadcasted_iota(jnp.int32, tail.shape, 2)
    tail = jnp.where((at_row == 0) & (at_lane < 3), tail, 0.0)
    mean_area = jnp.sum(jnp.sum(tail, axis=0), keepdims=True) / points_all

    c0 = math.sqrt(2.0 / math.pi)
    c1 = c0 * 0.044715

    def forward(m, _):
        first = pl.multiple_of(m * points, points)
        preact[...] = mm(edge_gr[...], table[m])

        for r in range(0, points, ROWS):
            x = preact[r : r + ROWS, :] + b_hidden[...]
            x2 = x * x
            t = jnp.tanh(x * (c0 + c1 * x2))
            half = 0.5 * x
            hidden[pl.ds(first + r, ROWS), :] = (half + half * t).astype(bf16)
            bend = half * (1.0 - t * t) * (c0 + (3.0 * c1) * x2)
            slope[pl.ds(first + r, ROWS), :] = (0.5 + 0.5 * t + bend).astype(bf16)

        pred[m] = mm(w_out_t[...], hidden[pl.ds(first, points), :], NT) + b_out[...]
        return 0

    lax.fori_loop(0, members, forward, 0)

    spread = spread_coef(members)
    dpred[var_rows:, :] = jnp.zeros((var_pad - var_rows, members * points), bf16)
    loss_sum = jnp.zeros((ROWS, LANES), f32)
    inverse_mean = 1.0 / mean_area
    for g in range(0, points, LANES):
        area = area_weight[:, g : g + LANES]

        def score(block, loss_sum, g=g, area=area):
            v = pl.multiple_of(block * ROWS, ROWS)
            p = [pred[m, pl.ds(v, ROWS), g : g + LANES] for m in range(members)]
            truth = targets[pl.ds(v, ROWS), g : g + LANES]
            weighting = var_weight[pl.ds(v, ROWS), :] * area
            fit = jnp.zeros((ROWS, LANES), f32)
            grads = []
            for m in range(members):
                d = p[m] - truth
                q = d * d + smooth_sq
                r = lax.rsqrt(q)
                fit = fit + q * r
                grads.append(d * r * (1.0 / members))
            pairs = jnp.zeros((ROWS, LANES), f32)
            apart = [jnp.zeros((ROWS, LANES), f32) for _ in range(members)]
            for j in range(members):
                for k in range(j + 1, members):
                    d = p[j] - p[k]
                    q = d * d + smooth_sq
                    r = lax.rsqrt(q)
                    pairs = pairs + q * r
                    s = d * r
                    apart[j] = apart[j] + s
                    apart[k] = apart[k] - s
            scaled = weighting * inverse_mean
            for m in range(members):
                gradient = grads[m] - (2.0 * spread) * apart[m]
                dpred[pl.ds(v, ROWS), m * points + g : m * points + g + LANES] = (
                    gradient * scaled
                ).astype(bf16)
            return loss_sum + weighting * (
                fit * (1.0 / members) - (2.0 * spread) * pairs
            )

        loss_sum = lax.fori_loop(0, var_rows // ROWS, score, loss_sum)
    loss = jnp.sum(loss_sum, keepdims=True) * (inverse_mean / points_all)

    for m in range(members):
        first = m * points
        grad = mm(dpred[:, first : first + points], w_out_t[...], TN)
        grad = (grad * slope[first : first + points, :].astype(f32)).astype(bf16)
        grad = mm(edge_rg[...], grad)
        for c in range(width // LANES):
            dtable[c, pl.ds(m, rows, stride=members), :] = grad[:, c * LANES : (c + 1) * LANES]

    own = mesh_rows * members
    for c in range(width // LANES):
        left, right = c * LANES, (c + 1) * LANES
        dlocal[:, left:right] = dtable[c, :own, :]
        dtable_low[:, left:right] = dtable[c].astype(bf16)
    slot_grad[...] = dtable_low[own:, :].reshape(shards, per_pair, width)

    half_width = width // 2
    pairs, _, own_rows, columns = partial.shape
    core = lax.rem(me, 2)
    for c, (keep, send) in enumerate(((keep_a, send_a), (keep_b, send_b))):
        left, right = c * half_width, (c + 1) * half_width
        grad = mm(latent[...], dtable_low[:own, left:right], TN)
        grad = grad + mm(arrived_rows, dtable_low[own:, left:right], TN)
        partial[:, :, :, :half_width] = grad.astype(bf16).reshape(
            pairs, 2, own_rows, half_width
        )
        if c == 0:
            grad = mm(dpred[...], hidden[...]).T
            row = lax.broadcasted_iota(jnp.int32, grad.shape, 0)
            lane = lax.broadcasted_iota(jnp.int32, grad.shape, 1)
            row = lax.rem(row, own_rows)
            grad = jnp.where(lane < variables, grad, 0.0)
            for i, piece in enumerate(split_sum(loss)[:2]):
                place = me * 2 + i
                here = (row == lax.rem(place, own_rows)) & (
                    lane == variables + place // own_rows
                )
                grad = jnp.where(here, piece.astype(f32), grad)
            partial[:, :, :, half_width:] = grad.astype(bf16).reshape(
                pairs, 2, own_rows, columns - half_width
            )
            keep[...] = partial[:, core]
            send[...] = partial[:, 1 - core]
        else:
            keep[...] = partial[:, core, :, :half_width]
            send[...] = partial[:, 1 - core, :, :half_width]


def latent_grad_kernel(rows_ref, returned, dlocal, w_src, out, selector, *, members, slots):
    shards, per_pair, width = returned.shape
    fill_selector(rows_ref, selector, shards, slots, members)
    back = returned[...].reshape(shards * per_pair, width)
    total = dlocal[...] + mm(selector[...].astype(bf16), back, TN)
    out[...] = mm(total.astype(bf16), w_src[...], NT)


def call(kernel, out_shape, in_specs, scratch, cost, *args):
    single = not isinstance(out_shape, (list, tuple))
    return pl.pallas_call(
        kernel,
        out_shape=out_shape,
        in_specs=in_specs,
        out_specs=VMEM if single else [VMEM] * len(out_shape),
        scratch_shapes=scratch,
        compiler_params=pltpu.CompilerParams(vmem_limit_bytes=VMEM_BYTES),
        cost_estimate=pl.CostEstimate(flops=cost, bytes_accessed=4 << 20, transcendentals=0),
    )(*args)


def halve(summed, bits, bit, me, shards):
    place = bits.index(bit)
    shape = summed.shape
    split = summed.reshape(1 << place, 2, -1, *shape[1:])
    mine = (me // bit) % 2
    keep = lax.dynamic_index_in_dim(split, mine, 1, keepdims=False)
    send = lax.dynamic_index_in_dim(split, 1 - mine, 1, keepdims=False)
    flat = (-1, *shape[1:])
    return keep.reshape(flat), send.reshape(flat)


def swap(value, bit, shards):
    return lax.ppermute(value, "space", [(i, i ^ bit) for i in range(shards)])


def per_device(
    latent,
    w_src,
    b_hidden,
    w_out,
    b_out,
    targets,
    var_weight,
    area_weight,
    edge_src,
    edge_coef,
    send_rows,
):
    mesh_rows, members, width = latent.shape
    shards = lax.axis_size("space")
    slots = send_rows.shape[2]
    variables, points = targets.shape
    points_all = points * shards
    own_rows = width // shards
    per_pair = slots * members
    rows = mesh_rows + shards * slots
    loss_columns = round_up(2 * shards, own_rows) // own_rows
    var_pad = round_up(variables + loss_columns, LANES)
    var_rows = round_up(variables, ROWS)
    half_width = width // 2
    shape = jax.ShapeDtypeStruct
    me = lax.axis_index("space").astype(jnp.int32)

    latent_rows = latent.reshape(mesh_rows * members, width)
    slot_rows = jnp.swapaxes(send_rows, 1, 2)
    area_row = area_weight.reshape(1, points)
    selector = pltpu.VMEM((shards * per_pair, mesh_rows * members), f32)
    outgoing = call(
        functools.partial(pack_kernel, members=members, slots=slots),
        shape((shards, per_pair, width + LANES), bf16),
        [SMEM, VMEM, VMEM],
        [selector],
        1 << 29,
        slot_rows,
        latent_rows,
        area_row,
    )
    arrived = lax.all_to_all(outgoing, "space", split_axis=0, concat_axis=0, tiled=True)

    local, edge_gr, edge_rg = call(
        functools.partial(local_kernel, members=members),
        [
            shape((members, mesh_rows, width), bf16),
            shape((points, rows), bf16),
            shape((rows, points), bf16),
        ],
        [VMEM] * 4,
        [pltpu.VMEM((width // LANES, mesh_rows * members, LANES), f32)],
        1 << 31,
        latent_rows,
        w_src,
        edge_src.T,
        edge_coef.T,
    )
    w_out_t = jnp.pad(w_out.T, ((0, var_pad - variables), (0, 0)))
    b_out_column = jnp.pad(b_out, (0, var_pad - variables)).reshape(var_pad, 1)
    var_column = jnp.pad(var_weight, (0, var_rows - variables)).reshape(var_rows, 1)
    targets_pad = jnp.pad(targets, ((0, var_rows - variables), (0, 0)))

    dlocal, slot_grad, keep_a, send_a, keep_b, send_b = call(
        functools.partial(decoder_kernel, points_all=points_all, variables=variables),
        [
            shape((mesh_rows * members, width), f32),
            shape((shards, per_pair, width), bf16),
            shape((shards // 2, own_rows, half_width + var_pad), bf16),
            shape((shards // 2, own_rows, half_width + var_pad), bf16),
            shape((shards // 2, own_rows, half_width), bf16),
            shape((shards // 2, own_rows, half_width), bf16),
        ],
        [SMEM] + [VMEM] * 12,
        [
            pltpu.VMEM((members, rows, width), bf16),
            pltpu.VMEM((members * points, width), bf16),
            pltpu.VMEM((members * points, width), bf16),
            pltpu.VMEM((points, width), f32),
            pltpu.VMEM((members, var_pad, points), f32),
            pltpu.VMEM((var_pad, members * points), bf16),
            pltpu.VMEM((width // LANES, rows * members, LANES), f32),
            pltpu.VMEM((rows * members, width), bf16),
            pltpu.VMEM((shards // 2, 2, own_rows, half_width + var_pad), bf16),
        ],
        1 << 34,
        me.reshape(1),
        arrived,
        local,
        latent_rows,
        w_src,
        edge_gr,
        edge_rg,
        b_hidden.reshape(1, width),
        w_out_t,
        b_out_column,
        targets_pad,
        var_column,
        area_row,
    )

    returned = lax.all_to_all(slot_grad, "space", split_axis=0, concat_axis=0, tiled=True)

    levels = [1 << i for i in reversed(range(1, shards.bit_length() - 1))]
    order_a = levels[::-1]
    order_b = order_a[1:2] + order_a[:1] + order_a[2:]
    got_a, got_b = swap(send_a, 1, shards), swap(send_b, 1, shards)
    bits_a, bits_b = list(levels), list(levels)
    for bit_a, bit_b in zip(order_a, order_b, strict=True):
        sum_a = (keep_a.astype(f32) + got_a.astype(f32)).astype(bf16)
        sum_b = (keep_b.astype(f32) + got_b.astype(f32)).astype(bf16)
        keep_a, send_a = halve(sum_a, bits_a, bit_a, me, shards)
        keep_b, send_b = halve(sum_b, bits_b, bit_b, me, shards)
        got_a, got_b = swap(send_a, bit_a, shards), swap(send_b, bit_b, shards)
        bits_a.remove(bit_a)
        bits_b.remove(bit_b)
    total_a = (keep_a.astype(f32) + got_a.astype(f32))[0]
    total_b = (keep_b.astype(f32) + got_b.astype(f32))[0]

    grad_latent = call(
        functools.partial(latent_grad_kernel, members=members, slots=slots),
        shape((mesh_rows * members, width), f32),
        [SMEM] + [VMEM] * 3,
        [selector],
        1 << 31,
        slot_rows,
        returned,
        dlocal,
        w_src,
    ).reshape(mesh_rows, members, width)

    grad_scale = WSCALE / points_all
    grad_w_src = jnp.concatenate([total_a[:, :half_width], total_b], axis=1) * grad_scale
    grad_w_out = total_a[:, half_width : half_width + variables] * grad_scale
    loss = jnp.sum(total_a[:, half_width + variables :]).reshape(1)
    return (loss, grad_latent, grad_w_src, grad_w_out)


def solution(mesh):
    placed = (
        P(("groups", "space"), None, None),
        P(),
        P(),
        P(),
        P(),
        P(None, ("groups", "space")),
        P(),
        P("space"),
        P("space", None),
        P("space", None),
        P("space", None, None),
    )
    return jax.shard_map(
        per_device,
        mesh=mesh,
        in_specs=placed,
        out_specs=(
            P("groups"),
            P(("groups", "space"), None, None),
            P(("groups", "space"), None),
            P(("groups", "space"), None),
        ),
        check_vma=False,
    )
```

```python
import functools
import math

import jax
import jax.numpy as jnp
from jax import lax
from jax.experimental import pallas as pl
from jax.experimental.pallas import tpu as pltpu
from jax.sharding import PartitionSpec as P

WSCALE = 2048
LANES = 128
ROWS = 16
alpha_fair = 0.95
smooth_sq = 0.01
MIB = 1 << 20

f32 = jnp.float32
bf16 = jnp.bfloat16
NN = (((1,), (0,)), ((), ()))
TN = (((0,), (0,)), ((), ()))
NT = (((1,), (1,)), ((), ()))
SMEM = pl.BlockSpec(memory_space=pltpu.SMEM)
VMEM = pl.BlockSpec(memory_space=pltpu.VMEM)
ANY = pl.BlockSpec(memory_space=pl.ANY)
HBM = pl.BlockSpec(memory_space=pltpu.HBM)


def spread_coef(members):
    return alpha_fair / (2.0 * members * (members - 1)) + (1.0 - alpha_fair) / (
        2.0 * members * members
    )


def mm(a, b, dims=NN):
    return lax.dot_general(a, b, dims, preferred_element_type=f32)


def round_up(value, multiple):
    return -(-value // multiple) * multiple


def split_sum(value):
    high = value.astype(bf16)
    rest = value - high.astype(f32)
    middle = rest.astype(bf16)
    return high, middle, (rest - middle.astype(f32)).astype(bf16)


def project(projected, rows, w_src):
    out = mm(rows, w_src[...])
    for c in range(projected.shape[0]):
        projected[c, : rows.shape[0], :] = out[:, c * LANES : (c + 1) * LANES]


def by_member(projected, table, first, count):
    members = table.shape[0]
    for m in range(members):
        for c in range(projected.shape[0]):
            block = projected[c, pl.ds(m, count, stride=members), :]
            table[m, first : first + count, c * LANES : (c + 1) * LANES] = block.astype(bf16)


def pack_kernel(rows_ref, latent, area, out, zeros, sem):
    shards, slots, members, _ = out.shape
    width = zeros.shape[1]
    zeros[...] = jnp.zeros_like(zeros)
    for s in range(shards):
        for b in range(slots):
            row = rows_ref[0, b, s]
            target = out.at[s, b, :, pl.ds(0, width)]

            @pl.when(row >= 0)
            def _(row=row, target=target):
                pltpu.make_async_copy(latent.at[row], target, sem).start()

            @pl.when(row < 0)
            def _(target=target):
                pltpu.make_async_copy(zeros, target, sem).start()

    total = jnp.sum(area[...], axis=1, keepdims=True) + jnp.zeros((members, LANES), f32)
    lane = lax.broadcasted_iota(jnp.int32, (members, LANES), 1)
    tail = jnp.zeros((members, LANES), f32)
    for i, piece in enumerate(split_sum(total)):
        tail = jnp.where(lane == i, piece.astype(f32), tail)
    tail = tail.astype(bf16)
    for s in range(shards):
        for b in range(slots):
            out[s, b, :, width:] = tail
    for s in range(shards):
        for b in range(slots):
            pltpu.make_async_copy(zeros, out.at[s, b, :, pl.ds(0, width)], sem).wait()


def local_kernel(
    latent,
    w_src,
    edge_src,
    edge_coef,
    b_hidden,
    w_out_t,
    b_out,
    targets,
    var_weight,
    area_weight,
    table,
    edge_gr,
    edge_rg,
    w_out_pad,
    w_out_t_pad,
    b_out_pad,
    truth,
    weighting,
    w_src_t,
    projected,
    wide,
    tall,
):
    members, rows_pad, width = table.shape
    rows, points = edge_rg.shape
    mesh_rows = latent.shape[0] // members
    variables = w_out_t.shape[0]
    project(projected, latent[...], w_src)
    by_member(projected, table, 0, mesh_rows)

    row = lax.broadcasted_iota(jnp.int32, (rows_pad, points), 0)
    matrix = jnp.where((row >= rows) & (row < rows + 2), 1.0, 0.0).astype(f32)
    for k in range(edge_src.shape[0]):
        matrix = matrix + jnp.where(
            row == edge_src[k : k + 1, :], edge_coef[k : k + 1, :], 0.0
        )
    edge_rg[...] = matrix[:rows].astype(bf16)
    edge_gr[...] = matrix.T.astype(bf16)

    bias = b_hidden[...]
    high, low, _ = split_sum(bias)
    at = lax.broadcasted_iota(jnp.int32, (rows_pad - rows, width), 0)
    bias_rows = jnp.where(
        at == 0, high.astype(f32), jnp.where(at == 1, low.astype(f32), 0.0)
    ).astype(bf16)
    for m in range(members):
        table[m, rows:, :] = bias_rows

    wide[...] = jnp.zeros_like(wide)
    wide[:variables, :] = w_out_t[...].astype(f32)
    w_out_t_pad[...] = wide[...].astype(bf16)
    w_out_pad[...] = wide[...].T.astype(bf16)
    tall[...] = jnp.zeros_like(tall)
    tall[:variables, :] = targets[...]
    truth[...] = tall[...].T
    b_out_pad[...] = jnp.zeros_like(b_out_pad)
    b_out_pad[:, :variables] = b_out[...]
    weighting[...] = jnp.zeros_like(weighting)
    column = jnp.broadcast_to(area_weight[...], (LANES, points)).T
    w_src_t[...] = w_src[...].T
    weighting[:, :variables] = column[:, :variables] * var_weight[...]


def decoder_kernel(
    me_ref,
    arrived,
    w_src_hbm,
    table_hbm,
    edge_gr_hbm,
    w_out_hbm,
    b_out_hbm,
    truth_hbm,
    weighting_hbm,
    w_out_t_hbm,
    edge_rg_hbm,
    latent_hbm,
    dlocal_hbm,
    slot_grad_hbm,
    keep_a,
    send_a,
    keep_b,
    send_b,
    w_src,
    table,
    edge_gr,
    w_out_pad,
    b_out_pad,
    truth,
    weighting,
    w_out_t_pad,
    edge_rg,
    latent,
    hidden,
    slope,
    preact,
    pred,
    dpred,
    dtable,
    dlocal,
    slot_grad,
    partial,
    partial_b,
    sem,
    *,
    points_all,
    variables,
):
    members, rows_pad, width = table.shape
    shards, per_pair, _ = arrived.shape
    received = shards * per_pair
    rows, points = edge_rg.shape
    own = latent.shape[0]
    mesh_rows = own // members
    var_pad = w_out_pad.shape[1]
    me = me_ref[0]

    sources = (
        w_src_hbm,
        table_hbm,
        edge_gr_hbm,
        w_out_hbm,
        b_out_hbm,
        truth_hbm,
        weighting_hbm,
        w_out_t_hbm,
        edge_rg_hbm,
        latent_hbm,
    )
    targets = (
        w_src,
        table,
        edge_gr,
        w_out_pad,
        b_out_pad,
        truth,
        weighting,
        w_out_t_pad,
        edge_rg,
        latent,
    )
    loads = [
        pltpu.make_async_copy(source, target, sem.at[i])
        for i, (source, target) in enumerate(zip(sources, targets, strict=True))
    ]
    loads[0].start()

    loads[0].wait()
    for load in loads[1:]:
        load.start()
    arrived_rows = arrived[:, :, :width].reshape(received, width)
    project(dtable, arrived_rows, w_src)
    loads[1].wait()
    by_member(dtable, table, mesh_rows, received // members)
    for load in loads[2:]:
        load.wait()

    tail = arrived[:, :, width:].astype(f32)
    at_row = lax.broadcasted_iota(jnp.int32, tail.shape, 1)
    at_lane = lax.broadcasted_iota(jnp.int32, tail.shape, 2)
    tail = jnp.where((at_row == 0) & (at_lane < 3), tail, 0.0)
    mean_area = jnp.sum(jnp.sum(tail, axis=0), keepdims=True) / points_all

    c0 = math.sqrt(2.0 / math.pi)
    c1 = c0 * 0.044715
    quarter = width // 4

    def gather(m, slot, c):
        left, right = c * quarter, (c + 1) * quarter
        preact[slot, :, left:right] = mm(edge_gr[...], table[m, :, left:right])

    for c in range(4):
        gather(0, 0, c)

    def forward(pair, _):
        for slot in range(2):
            m = pair * 2 + slot
            first = pl.multiple_of(m * points, points)
            following = jnp.minimum(m + 1, members - 1)
            for c in range(4):
                left, right = c * quarter, (c + 1) * quarter
                gather(following, 1 - slot, c)
                for r in range(0, points, ROWS):
                    x = preact[slot, r : r + ROWS, left:right]
                    x2 = x * x
                    t = jnp.tanh(x * (c0 + c1 * x2))
                    cdf = 0.5 + 0.5 * t
                    hidden[pl.ds(first + r, ROWS), left:right] = (x * cdf).astype(bf16)
                    bend = (1.0 - t) * (x * (c0 + (3.0 * c1) * x2)) + 1.0
                    slope[pl.ds(first + r, ROWS), left:right] = (cdf * bend).astype(bf16)
            pred[m] = mm(hidden[pl.ds(first, points), :], w_out_pad[...]) + b_out_pad[...]
        return 0

    lax.fori_loop(0, members // 2, forward, 0)

    spread = spread_coef(members)
    inverse_mean = 1.0 / mean_area
    loss_sum = jnp.zeros((ROWS, LANES), f32)
    for left in range(0, var_pad, LANES):

        def score(block, loss_sum, left=left):
            at = pl.ds(pl.multiple_of(block * ROWS, ROWS), ROWS)
            p = [pred[m, at, left : left + LANES] for m in range(members)]
            true = truth[at, left : left + LANES]
            weight = weighting[at, left : left + LANES]
            fit = jnp.zeros((ROWS, LANES), f32)
            grads = []
            for m in range(members):
                d = p[m] - true
                q = d * d + smooth_sq
                r = lax.rsqrt(q)
                fit = fit + q * r
                grads.append(d * r * (1.0 / members))
            pairs = jnp.zeros((ROWS, LANES), f32)
            apart = [jnp.zeros((ROWS, LANES), f32) for _ in range(members)]
            for j in range(members):
                for k in range(j + 1, members):
                    d = p[j] - p[k]
                    q = d * d + smooth_sq
                    r = lax.rsqrt(q)
                    pairs = pairs + q * r
                    s = d * r
                    apart[j] = apart[j] + s
                    apart[k] = apart[k] - s
            scaled = weight * inverse_mean
            for m in range(members):
                gradient = grads[m] - (2.0 * spread) * apart[m]
                dpred[m, at, left : left + LANES] = (gradient * scaled).astype(bf16)
            return loss_sum + weight * (fit * (1.0 / members) - (2.0 * spread) * pairs)

        loss_sum = lax.fori_loop(0, points // ROWS, score, loss_sum)
    loss = jnp.sum(loss_sum, keepdims=True) * (inverse_mean / points_all)

    for m in range(members):
        first = m * points
        grad = mm(dpred[m], w_out_t_pad[...])
        grad = (grad * slope[first : first + points, :].astype(f32)).astype(bf16)
        grad = mm(edge_rg[...], grad)
        for c in range(width // LANES):
            dtable[c, pl.ds(m, rows, stride=members), :] = grad[:, c * LANES : (c + 1) * LANES]

    for c in range(width // LANES):
        left, right = c * LANES, (c + 1) * LANES
        dlocal[:, left:right] = dtable[c, :own, :].astype(bf16)
        slot_grad[:, :, left:right] = (
            dtable[c, own:, :].astype(bf16).reshape(shards, per_pair, LANES)
        )
    stores = [
        pltpu.make_async_copy(slot_grad, slot_grad_hbm, sem.at[0]),
        pltpu.make_async_copy(dlocal, dlocal_hbm, sem.at[1]),
    ]
    for store in stores:
        store.start()

    half_width = width // 2
    pairs, _, own_rows, columns = partial.shape
    core = lax.rem(me, 2)
    grad = mm(dpred[...].reshape(members * points, var_pad), hidden[...], TN).T
    row = lax.broadcasted_iota(jnp.int32, grad.shape, 0)
    lane = lax.broadcasted_iota(jnp.int32, grad.shape, 1)
    row = row & (own_rows - 1)
    grad = jnp.where(lane < variables, grad, 0.0)
    for i, piece in enumerate(split_sum(loss)[:2]):
        place = me * 2 + i
        here = (row == lax.rem(place, own_rows)) & (lane == variables + place // own_rows)
        grad = jnp.where(here, piece.astype(f32), grad)
    partial[:, :, :, half_width:] = grad.astype(bf16).reshape(
        pairs, 2, own_rows, columns - half_width
    )
    back = slot_grad[...].reshape(received, width)
    for c, (keep, send) in enumerate(((keep_a, send_a), (keep_b, send_b))):
        left, right = c * half_width, (c + 1) * half_width
        grad = mm(latent[...], dlocal[:, left:right], TN)
        grad = grad + mm(arrived_rows, back[:, left:right], TN)
        part = partial if c == 0 else partial_b
        part[:, :, :, :half_width] = grad.astype(bf16).reshape(
            pairs, 2, own_rows, half_width
        )
        for i, (half, target) in enumerate(((1 - core, send), (core, keep))):
            stores.append(pltpu.make_async_copy(part.at[:, half], target, sem.at[2 + 2 * c + i]))
            stores[-1].start()
    for store in stores:
        store.wait()


def halve_kernel(me_ref, keep_a, got_a, keep_b, got_b, *rest, bits):
    outs = rest[-4:]
    for i, (keep, got, bit) in enumerate(
        ((keep_a, got_a, bits[0]), (keep_b, got_b, bits[1]))
    ):
        mine = lax.rem(me_ref[0] // bit, 2)
        for out, half in ((outs[2 * i + 1], 1 - mine), (outs[2 * i], mine)):
            total = keep[:, half].astype(f32) + got[:, half].astype(f32)
            out[...] = total.astype(bf16)


def final_kernel(keep_a, got_a, keep_b, got_b, grad_w_src, grad_w_out, loss, *, scale):
    variables = grad_w_out.shape[1]
    half_width = grad_w_src.shape[1] // 2
    total = keep_a[0].astype(f32) + got_a[0].astype(f32)
    grad_w_src[:, :half_width] = total[:, :half_width] * scale
    grad_w_src[:, half_width:] = (keep_b[0].astype(f32) + got_b[0].astype(f32)) * scale
    out = total[:, half_width:]
    grad_w_out[...] = out[:, :variables] * scale
    lane = lax.broadcasted_iota(jnp.int32, out.shape, 1)
    loss[...] = jnp.sum(jnp.where(lane >= variables, out, 0.0), keepdims=True)


def latent_grad_kernel(
    rows_ref, returned, dlocal_hbm, w_src_t_hbm, _, out_hbm, selector, dlocal, w_src_t, out, sem
):
    shards, per_pair, width = returned.shape
    _, slots, _ = rows_ref.shape
    members = per_pair // slots
    loads = [
        pltpu.make_async_copy(w_src_t_hbm, w_src_t, sem.at[0]),
        pltpu.make_async_copy(dlocal_hbm, dlocal, sem.at[1]),
    ]
    for load in loads:
        load.start()
    lane = lax.broadcasted_iota(jnp.int32, (members, selector.shape[1]), 1)
    member = lax.broadcasted_iota(jnp.int32, (members, selector.shape[1]), 0)
    for s in range(shards):
        for b in range(slots):
            first = (s * slots + b) * members
            selector[first : first + members, :] = jnp.where(
                lane == rows_ref[0, b, s] * members + member, 1.0, 0.0
            ).astype(f32)
    back = returned[...].reshape(shards * per_pair, width)
    spread = mm(selector[...].astype(bf16), back, TN)
    for load in loads:
        load.wait()
    total = (dlocal[...].astype(f32) + spread).astype(bf16)
    stores = []
    chunk = width // 4
    for i in range(4):
        part = pl.ds(i * chunk, chunk)
        out[:, part] = mm(total, w_src_t[:, part])
        stores.append(
            pltpu.make_async_copy(out.at[:, part], out_hbm.at[:, part], sem.at[2 + i])
        )
        stores[-1].start()
    for store in stores:
        store.wait()


def size_of(x):
    return math.prod(x.shape) * jnp.dtype(x.dtype).itemsize


def call(kernel, out_shape, in_specs, scratch, cost, *args, out_specs=None, limit=None):
    single = not isinstance(out_shape, (list, tuple))
    outs = [out_shape] if single else list(out_shape)
    specs = out_specs or [VMEM] * len(outs)
    used = sum(size_of(x) for x, s in zip(args, in_specs, strict=True) if s is VMEM)
    used += sum(size_of(x) for x, s in zip(outs, specs, strict=True) if s is VMEM)
    used += sum(size_of(x) for x in scratch if getattr(x, "dtype", None) in (f32, bf16))
    limit = min(limit or used + used // 4 + 6 * MIB, 60 * MIB)
    return pl.pallas_call(
        kernel,
        out_shape=out_shape,
        in_specs=in_specs,
        out_specs=specs[0] if single else specs,
        scratch_shapes=scratch,
        compiler_params=pltpu.CompilerParams(vmem_limit_bytes=limit),
        cost_estimate=pl.CostEstimate(flops=cost, bytes_accessed=used, transcendentals=0),
    )(*args)


def swap(value, bit, shards):
    return lax.ppermute(value, "space", [(i, i ^ bit) for i in range(shards)])


def per_device(
    latent,
    w_src,
    b_hidden,
    w_out,
    b_out,
    targets,
    var_weight,
    area_weight,
    edge_src,
    edge_coef,
    send_rows,
):
    mesh_rows, members, width = latent.shape
    shards = lax.axis_size("space")
    slots = send_rows.shape[2]
    variables, points = targets.shape
    points_all = points * shards
    own_rows = width // shards
    per_pair = slots * members
    rows = mesh_rows + shards * slots
    rows_pad = round_up(rows + 2, ROWS)
    loss_columns = round_up(2 * shards, own_rows) // own_rows
    var_pad = round_up(variables + loss_columns, LANES)
    half_width = width // 2
    shape = jax.ShapeDtypeStruct
    me = lax.axis_index("space").astype(jnp.int32).reshape(1)

    latent_rows = latent.reshape(mesh_rows * members, width)
    slot_rows = jnp.swapaxes(send_rows, 1, 2)
    area_row = area_weight.reshape(1, points)
    outgoing = call(
        pack_kernel,
        shape((shards, slots, members, width + LANES), bf16),
        [SMEM, ANY, VMEM],
        [pltpu.VMEM((members, width), bf16), pltpu.SemaphoreType.DMA],
        1 << 24,
        slot_rows,
        latent,
        area_row,
        limit=56 * MIB,
    )
    arrived = lax.all_to_all(outgoing, "space", split_axis=0, concat_axis=0, tiled=True)
    arrived = arrived.reshape(shards, per_pair, width + LANES)

    columns = (half_width + var_pad, half_width)
    table, edge_gr, edge_rg, w_out_pad, w_out_t_pad, b_out_pad, truth, weighting, w_src_t = call(
        local_kernel,
        [
            shape((members, rows_pad, width), bf16),
            shape((points, rows_pad), bf16),
            shape((rows, points), bf16),
            shape((width, var_pad), bf16),
            shape((var_pad, width), bf16),
            shape((1, var_pad), f32),
            shape((points, var_pad), f32),
            shape((points, var_pad), f32),
            shape((width, width), bf16),
        ],
        [VMEM] * 10,
        [
            pltpu.VMEM((width // LANES, mesh_rows * members, LANES), f32),
            pltpu.VMEM((var_pad, width), f32),
            pltpu.VMEM((var_pad, points), f32),
        ],
        1 << 31,
        latent_rows,
        w_src,
        edge_src.T,
        edge_coef.T,
        b_hidden.reshape(1, width),
        w_out.T,
        b_out.reshape(1, variables),
        targets,
        var_weight.reshape(1, variables),
        area_row,
        limit=56 * MIB,
    )

    operands = (
        w_src,
        table,
        edge_gr,
        w_out_pad,
        b_out_pad,
        truth,
        weighting,
        w_out_t_pad,
        edge_rg,
        latent_rows,
    )
    dlocal, slot_grad, *pieces = call(
        functools.partial(decoder_kernel, points_all=points_all, variables=variables),
        [
            shape((mesh_rows * members, width), bf16),
            shape((shards, per_pair, width), bf16),
            *[shape((shards // 2, own_rows, n), bf16) for n in columns for _ in range(2)],
        ],
        [SMEM, VMEM] + [HBM] * len(operands),
        [
            *[pltpu.VMEM(x.shape, x.dtype) for x in operands],
            pltpu.VMEM((members * points, width), bf16),
            pltpu.VMEM((members * points, width), bf16),
            pltpu.VMEM((2, points, width), f32),
            pltpu.VMEM((members, points, var_pad), f32),
            pltpu.VMEM((members, points, var_pad), bf16),
            pltpu.VMEM((width // LANES, rows * members, LANES), f32),
            pltpu.VMEM((mesh_rows * members, width), bf16),
            pltpu.VMEM((shards, per_pair, width), bf16),
            pltpu.VMEM((shards // 2, 2, own_rows, columns[0]), bf16),
            pltpu.VMEM((shards // 2, 2, own_rows, columns[1]), bf16),
            pltpu.SemaphoreType.DMA((len(operands),)),
        ],
        1 << 34,
        me,
        arrived,
        *operands,
        out_specs=[HBM] * 6,
        limit=56 * MIB,
    )

    returned = lax.all_to_all(slot_grad, "space", split_axis=0, concat_axis=0, tiled=True)

    levels = [1 << i for i in reversed(range(1, shards.bit_length() - 1))]
    order_a = levels[::-1]
    order_b = order_a[1:2] + order_a[:1] + order_a[2:]
    left = [list(levels), list(levels)]
    count = shards // 2
    got = [swap(pieces[1], 1, shards), swap(pieces[3], 1, shards)]
    for step, bits in enumerate(zip(order_a, order_b, strict=True)):
        views = []
        for i, bit in enumerate(bits):
            place = left[i].index(bit)
            left[i].remove(bit)
            split = (1 << place, 2, count >> (place + 1), own_rows, columns[i])
            views += [pieces[2 * i].reshape(split), got[i].reshape(split)]
        count //= 2
        halves = [(x.shape[0], *x.shape[2:]) for x in views[::2] for _ in range(2)]
        pieces = call(
            functools.partial(halve_kernel, bits=bits),
            [shape(x, bf16) for x in halves],
            [SMEM] + [VMEM] * len(views),
            [],
            1 << 24,
            me,
            *views,
        )
        pieces = [x.reshape(count, *x.shape[2:]) for x in pieces]
        got = [swap(pieces[2 * i + 1], bit, shards) for i, bit in enumerate(bits)]

    grad_latent = call(
        latent_grad_kernel,
        shape((mesh_rows * members, width), f32),
        [SMEM, VMEM, HBM, HBM, ANY],
        [
            pltpu.VMEM((shards * per_pair, mesh_rows * members), f32),
            pltpu.VMEM((mesh_rows * members, width), bf16),
            pltpu.VMEM((width, width), bf16),
            pltpu.VMEM((mesh_rows * members, width), f32),
            pltpu.SemaphoreType.DMA((6,)),
        ],
        1 << 32,
        slot_rows,
        returned,
        dlocal,
        w_src_t,
        pieces[0],
        out_specs=[HBM],
        limit=56 * MIB,
    )
    grad_w_src, grad_w_out, loss = call(
        functools.partial(final_kernel, scale=WSCALE / points_all),
        [
            shape((own_rows, width), f32),
            shape((own_rows, variables), f32),
            shape((1, 1), f32),
        ],
        [VMEM] * 4,
        [],
        1 << 24,
        pieces[0],
        got[0],
        pieces[2],
        got[1],
    )
    return (
        loss.reshape(1),
        grad_latent.reshape(mesh_rows, members, width),
        grad_w_src,
        grad_w_out,
    )


def solution(mesh):
    placed = (
        P(("groups", "space"), None, None),
        P(),
        P(),
        P(),
        P(),
        P(None, ("groups", "space")),
        P(),
        P("space"),
        P("space", None),
        P("space", None),
        P("space", None, None),
    )
    return jax.shard_map(
        per_device,
        mesh=mesh,
        in_specs=placed,
        out_specs=(
            P("groups"),
            P(("groups", "space"), None, None),
            P(("groups", "space"), None),
            P(("groups", "space"), None),
        ),
        check_vma=False,
    )
```

```python
import functools
import math

import jax
import jax.numpy as jnp
from jax import lax
from jax.experimental import pallas as pl
from jax.experimental.pallas import tpu as pltpu
from jax.sharding import PartitionSpec as P

WSCALE = 2048
LANES = 128
ROWS = 16
alpha_fair = 0.95
smooth_sq = 0.01
MIB = 1 << 20
KEEP = 50
PACK = 56
UNROLL = 2

f32 = jnp.float32
bf16 = jnp.bfloat16
NN = (((1,), (0,)), ((), ()))
TN = (((0,), (0,)), ((), ()))
NT = (((1,), (1,)), ((), ()))
SMEM = pl.BlockSpec(memory_space=pltpu.SMEM)
VMEM = pl.BlockSpec(memory_space=pltpu.VMEM)
ANY = pl.BlockSpec(memory_space=pl.ANY)
HBM = pl.BlockSpec(memory_space=pltpu.HBM)


def spread_coef(members):
    return alpha_fair / (2.0 * members * (members - 1)) + (1.0 - alpha_fair) / (
        2.0 * members * members
    )


def mm(a, b, dims=NN):
    return lax.dot_general(a, b, dims, preferred_element_type=f32)


def round_up(value, multiple):
    return -(-value // multiple) * multiple


def split_sum(value):
    high = value.astype(bf16)
    rest = value - high.astype(f32)
    middle = rest.astype(bf16)
    return high, middle, (rest - middle.astype(f32)).astype(bf16)


def project(projected, rows, w_src):
    out = mm(rows, w_src[...])
    for c in range(projected.shape[0]):
        projected[c, : rows.shape[0], :] = out[:, c * LANES : (c + 1) * LANES]


def by_member(projected, table, members, rows_pad, first, count):
    for m in range(members):
        at = m * rows_pad + first
        for c in range(projected.shape[0]):
            block = projected[c, pl.ds(m, count, stride=members), :]
            table[at : at + count, c * LANES : (c + 1) * LANES] = block.astype(bf16)


def pack_kernel(rows_ref, latent, area, out, zeros, sem):
    shards, slots, members, _ = out.shape
    width = zeros.shape[1]
    zeros[...] = jnp.zeros_like(zeros)
    for s in range(shards):
        for b in range(slots):
            row = rows_ref[0, b, s]
            target = out.at[s, b, :, pl.ds(0, width)]

            @pl.when(row >= 0)
            def _(row=row, target=target):
                pltpu.make_async_copy(latent.at[row], target, sem).start()

            @pl.when(row < 0)
            def _(target=target):
                pltpu.make_async_copy(zeros, target, sem).start()

    total = jnp.sum(area[...], axis=1, keepdims=True) + jnp.zeros((members, LANES), f32)
    lane = lax.broadcasted_iota(jnp.int32, (members, LANES), 1)
    tail = jnp.zeros((members, LANES), f32)
    for i, piece in enumerate(split_sum(total)):
        tail = jnp.where(lane == i, piece.astype(f32), tail)
    tail = tail.astype(bf16)
    for s in range(shards):
        for b in range(slots):
            out[s, b, :, width:] = tail
    for s in range(shards):
        for b in range(slots):
            pltpu.make_async_copy(zeros, out.at[s, b, :, pl.ds(0, width)], sem).wait()


def strips(widths, width):
    places, strip, first = [], 0, 0
    for w in widths:
        if first + w > width:
            strip, first = strip + 1, 0
        places.append((strip, first))
        first += w
    return places, strip + 1


class Layout:
    def __init__(self, members, rows, points, var_pad, width):
        self.rows_pad = round_up(rows + 2, ROWS)
        self.out_first = members * self.rows_pad
        self.point_first = self.out_first + var_pad
        widths = [var_pad] * 6 + [round_up(self.rows_pad, LANES)]
        self.places, count = strips(widths, width)
        self.points = points
        self.edge_first = self.point_first + count * points
        self.shape = (self.edge_first + rows, width)

    def point_block(self, ref, i, columns):
        strip, first = self.places[i]
        at = self.point_first + strip * self.points
        return ref.at[pl.ds(at, self.points), pl.ds(first, columns)]


def local_kernel(
    latent,
    w_src,
    edge_src,
    edge_coef,
    b_hidden,
    w_out_t,
    b_out,
    targets,
    var_weight,
    area_weight,
    prepared,
    w_src_t,
    projected,
    wide,
    tall,
    *,
    layout,
    rows,
):
    variables, width = w_out_t.shape
    points = edge_src.shape[1]
    rows_pad = layout.rows_pad
    members = layout.out_first // rows_pad
    mesh_rows = latent.shape[0] // members
    var_pad = wide.shape[0]
    project(projected, latent[...], w_src)
    by_member(projected, prepared, members, rows_pad, 0, mesh_rows)

    row = lax.broadcasted_iota(jnp.int32, (rows_pad, points), 0)
    matrix = jnp.where((row >= rows) & (row < rows + 2), 0.5, 0.0).astype(f32)
    for k in range(edge_src.shape[0]):
        matrix = matrix + jnp.where(
            row == edge_src[k : k + 1, :], 0.5 * edge_coef[k : k + 1, :], 0.0
        )
    prepared[layout.edge_first :, :points] = matrix[:rows].astype(bf16)
    layout.point_block(prepared, 6, rows_pad)[...] = matrix.T.astype(bf16)

    high, low, _ = split_sum(b_hidden[...])
    at = lax.broadcasted_iota(jnp.int32, (rows_pad - rows, width), 0)
    bias_rows = jnp.where(
        at == 0, high.astype(f32), jnp.where(at == 1, low.astype(f32), 0.0)
    ).astype(bf16)
    for m in range(members):
        prepared[m * rows_pad + rows : (m + 1) * rows_pad, :] = bias_rows

    wide[...] = jnp.zeros_like(wide)
    wide[:variables, :] = w_out_t[...].astype(f32)
    prepared[layout.out_first : layout.point_first, :] = wide[...].astype(bf16)

    for i, value in ((0, targets[...] - b_out[...]), (3, var_weight[...] * area_weight[...])):
        tall[...] = jnp.zeros_like(tall)
        tall[:variables, :] = value
        for j, piece in enumerate(split_sum(tall[...].T)):
            layout.point_block(prepared, i + j, var_pad)[...] = piece
    w_src_t[...] = w_src[...].T


def decoder_kernel(
    me_ref,
    arrived,
    w_src_hbm,
    prepared_hbm,
    latent_hbm,
    dlocal_hbm,
    slot_grad_hbm,
    keep_a,
    send_a,
    keep_b,
    send_b,
    w_src,
    prepared,
    latent,
    hidden,
    slope,
    preact,
    pred,
    dpred,
    truth,
    weighting,
    w_out_pad,
    dtable,
    dlocal,
    slot_grad,
    sem,
    *,
    layout,
    points_all,
    variables,
):
    shards, per_pair, _ = arrived.shape
    received = shards * per_pair
    own, width = latent.shape
    members, points, var_pad = pred.shape
    mesh_rows = own // members
    rows = mesh_rows + received // members
    rows_pad = layout.rows_pad
    me = me_ref[0]

    loads = [
        pltpu.make_async_copy(source, target, sem.at[i])
        for i, (source, target) in enumerate(
            ((w_src_hbm, w_src), (prepared_hbm, prepared), (latent_hbm, latent))
        )
    ]
    for load in loads:
        load.start()

    loads[0].wait()
    arrived_rows = arrived[:, :, :width].reshape(received, width)
    project(dtable, arrived_rows, w_src)
    loads[1].wait()
    by_member(dtable, prepared, members, rows_pad, mesh_rows, received // members)
    w_out_t_pad = prepared[layout.out_first : layout.point_first, :]
    w_out_pad[...] = w_out_t_pad.T
    for i, target in ((0, truth), (3, weighting)):
        target[...] = sum(
            layout.point_block(prepared, i + j, var_pad)[...].astype(f32) for j in range(3)
        )

    tail = arrived[:, :, width:].astype(f32)
    at_row = lax.broadcasted_iota(jnp.int32, tail.shape, 1)
    at_lane = lax.broadcasted_iota(jnp.int32, tail.shape, 2)
    tail = jnp.where((at_row == 0) & (at_lane < 3), tail, 0.0)
    mean_area = jnp.sum(jnp.sum(tail, axis=0), keepdims=True) / points_all

    c0 = math.sqrt(2.0 / math.pi)
    c1 = c0 * 0.044715
    quarter = width // 4

    def gather(m, slot, c):
        left, right = c * quarter, (c + 1) * quarter
        table = prepared[pl.ds(pl.multiple_of(m * rows_pad, ROWS), rows_pad), left:right]
        preact[slot, :, left:right] = mm(layout.point_block(prepared, 6, rows_pad)[...], table)

    for c in range(4):
        gather(0, 0, c)

    def forward(pair, _):
        for slot in range(2):
            m = pair * 2 + slot
            first = pl.multiple_of(m * points, points)
            following = jnp.minimum(m + 1, members - 1)
            for c in range(4):
                left, right = c * quarter, (c + 1) * quarter
                gather(following, 1 - slot, c)
                for r in range(0, points, ROWS):
                    y = preact[slot, r : r + ROWS, left:right]
                    y2 = y * y
                    t = jnp.tanh(y * (2.0 * c0 + (8.0 * c1) * y2))
                    p = 1.0 + t
                    gelu = y * p
                    hidden[pl.ds(first + r, ROWS), left:right] = gelu.astype(bf16)
                    bend = (gelu * (1.0 - t)) * (2.0 * c0 + (24.0 * c1) * y2)
                    slope[pl.ds(first + r, ROWS), left:right] = (p + bend).astype(bf16)
            pred[m] = mm(hidden[pl.ds(first, points), :], w_out_pad[...])
        return 0

    lax.fori_loop(0, members // 2, forward, 0)

    spread = spread_coef(members)
    inverse_mean = 1.0 / mean_area
    loss_sum = jnp.zeros((ROWS, LANES), f32)
    for left in range(0, var_pad, LANES):

        def score(block, loss_sum, left=left):
            at = pl.ds(pl.multiple_of(block * ROWS, ROWS), ROWS)
            p = [pred[m, at, left : left + LANES] for m in range(members)]
            true = truth[at, left : left + LANES]
            weight = weighting[at, left : left + LANES]
            fit = jnp.zeros((ROWS, LANES), f32)
            grads = []
            for m in range(members):
                d = p[m] - true
                q = d * d + smooth_sq
                r = lax.rsqrt(q)
                fit = fit + q * r
                grads.append(d * r * (1.0 / members))
            pairs = jnp.zeros((ROWS, LANES), f32)
            apart = [jnp.zeros((ROWS, LANES), f32) for _ in range(members)]
            for j in range(members):
                for k in range(j + 1, members):
                    d = p[j] - p[k]
                    q = d * d + smooth_sq
                    r = lax.rsqrt(q)
                    pairs = pairs + q * r
                    s = d * r
                    apart[j] = apart[j] + s
                    apart[k] = apart[k] - s
            scaled = weight * inverse_mean
            for m in range(members):
                gradient = grads[m] - (2.0 * spread) * apart[m]
                dpred[m, at, left : left + LANES] = (gradient * scaled).astype(bf16)
            return loss_sum + weight * (fit * (1.0 / members) - (2.0 * spread) * pairs)

        loss_sum = lax.fori_loop(0, points // ROWS, score, loss_sum, unroll=UNROLL)
    loss = jnp.sum(loss_sum, keepdims=True) * (inverse_mean / points_all)

    for m in range(members):
        first = m * points
        grad = mm(dpred[m], w_out_t_pad)
        grad = (grad * slope[first : first + points, :].astype(f32)).astype(bf16)
        grad = mm(prepared[layout.edge_first :, :points], grad)
        for c in range(width // LANES):
            dtable[c, pl.ds(m, rows, stride=members), :] = grad[:, c * LANES : (c + 1) * LANES]

    for c in range(width // LANES):
        left, right = c * LANES, (c + 1) * LANES
        dlocal[:, left:right] = dtable[c, :own, :].astype(bf16)
        slot_grad[:, :, left:right] = (
            dtable[c, own:, :].astype(bf16).reshape(shards, per_pair, LANES)
        )
    stores = [
        pltpu.make_async_copy(slot_grad, slot_grad_hbm, sem.at[0]),
        pltpu.make_async_copy(dlocal, dlocal_hbm, sem.at[1]),
    ]
    for store in stores:
        store.start()

    half_width = width // 2
    pairs, own_rows, columns = keep_a.shape
    core = lax.rem(me, 2)
    grad = mm(dpred[...].reshape(members * points, var_pad), hidden[...], TN).T
    row = lax.broadcasted_iota(jnp.int32, grad.shape, 0)
    lane = lax.broadcasted_iota(jnp.int32, grad.shape, 1)
    row = row & (own_rows - 1)
    grad = jnp.where(lane < variables, grad, 0.0)
    for i, piece in enumerate(split_sum(loss)[:2]):
        place = me * 2 + i
        here = (row == lax.rem(place, own_rows)) & (lane == variables + place // own_rows)
        grad = jnp.where(here, piece.astype(f32), grad)
    out = grad.astype(bf16).reshape(pairs, 2, own_rows, columns - half_width)
    keep_a[:, :, half_width:] = jnp.where(core == 0, out[:, 0], out[:, 1])
    send_a[:, :, half_width:] = jnp.where(core == 0, out[:, 1], out[:, 0])
    loads[2].wait()
    back = slot_grad[...].reshape(received, width)
    for c, (keep, send) in enumerate(((keep_a, send_a), (keep_b, send_b))):
        left, right = c * half_width, (c + 1) * half_width
        grad = mm(latent[...], dlocal[:, left:right], TN)
        grad = grad + mm(arrived_rows, back[:, left:right], TN)
        grad = grad.astype(bf16).reshape(pairs, 2, own_rows, half_width)
        keep[:, :, :half_width] = jnp.where(core == 0, grad[:, 0], grad[:, 1])
        send[:, :, :half_width] = jnp.where(core == 0, grad[:, 1], grad[:, 0])
    for store in stores:
        store.wait()


def halve_kernel(me_ref, keep_a, got_a, keep_b, got_b, *rest, bits):
    outs = rest[-4:]
    for i, (keep, got, bit) in enumerate(
        ((keep_a, got_a, bits[0]), (keep_b, got_b, bits[1]))
    ):
        mine = lax.rem(me_ref[0] // bit, 2)
        for out, half in ((outs[2 * i + 1], 1 - mine), (outs[2 * i], mine)):
            total = keep[:, half].astype(f32) + got[:, half].astype(f32)
            out[...] = total.astype(bf16)


def final_kernel(keep_a, got_a, keep_b, got_b, grad_w_src, grad_w_out, loss, *, scale):
    variables = grad_w_out.shape[1]
    half_width = grad_w_src.shape[1] // 2
    total = keep_a[0].astype(f32) + got_a[0].astype(f32)
    grad_w_src[:, :half_width] = total[:, :half_width] * scale
    grad_w_src[:, half_width:] = (keep_b[0].astype(f32) + got_b[0].astype(f32)) * scale
    out = total[:, half_width:]
    grad_w_out[...] = out[:, :variables] * scale
    lane = lax.broadcasted_iota(jnp.int32, out.shape, 1)
    loss[...] = jnp.sum(jnp.where(lane >= variables, out, 0.0), keepdims=True)


def latent_grad_kernel(
    rows_ref, returned, dlocal_hbm, w_src_t_hbm, _, out_hbm, selector, dlocal, w_src_t, out, sem
):
    shards, per_pair, width = returned.shape
    _, slots, _ = rows_ref.shape
    members = per_pair // slots
    loads = [
        pltpu.make_async_copy(w_src_t_hbm, w_src_t, sem.at[0]),
        pltpu.make_async_copy(dlocal_hbm, dlocal, sem.at[1]),
    ]
    for load in loads:
        load.start()
    lane = lax.broadcasted_iota(jnp.int32, (members, selector.shape[1]), 1)
    member = lax.broadcasted_iota(jnp.int32, (members, selector.shape[1]), 0)
    for s in range(shards):
        for b in range(slots):
            first = (s * slots + b) * members
            selector[first : first + members, :] = jnp.where(
                lane == rows_ref[0, b, s] * members + member, 1.0, 0.0
            ).astype(f32)
    back = returned[...].reshape(shards * per_pair, width)
    spread = mm(selector[...].astype(bf16), back, TN)
    for load in loads:
        load.wait()
    total = (dlocal[...].astype(f32) + spread).astype(bf16)
    stores = []
    chunk = width // 4
    for i in range(4):
        part = pl.ds(i * chunk, chunk)
        out[:, part] = mm(total, w_src_t[:, part])
        stores.append(
            pltpu.make_async_copy(out.at[:, part], out_hbm.at[:, part], sem.at[2 + i])
        )
        stores[-1].start()
    for store in stores:
        store.wait()


def size_of(x):
    return math.prod(x.shape) * jnp.dtype(x.dtype).itemsize


def call(kernel, out_shape, in_specs, scratch, cost, *args, out_specs=None, limit=None):
    single = not isinstance(out_shape, (list, tuple))
    outs = [out_shape] if single else list(out_shape)
    specs = out_specs or [VMEM] * len(outs)
    used = sum(size_of(x) for x, s in zip(args, in_specs, strict=True) if s is VMEM)
    used += sum(size_of(x) for x, s in zip(outs, specs, strict=True) if s is VMEM)
    used += sum(size_of(x) for x in scratch if getattr(x, "dtype", None) in (f32, bf16))
    limit = limit or used + used // 4 + 6 * MIB
    if used > limit * 4 // 5:
        limit = 60 * MIB
    return pl.pallas_call(
        kernel,
        out_shape=out_shape,
        in_specs=in_specs,
        out_specs=specs[0] if single else specs,
        scratch_shapes=scratch,
        compiler_params=pltpu.CompilerParams(vmem_limit_bytes=limit),
        cost_estimate=pl.CostEstimate(flops=cost, bytes_accessed=used, transcendentals=0),
    )(*args)


def swap(value, bit, shards):
    return lax.ppermute(value, "space", [(i, i ^ bit) for i in range(shards)])


def per_device(
    latent,
    w_src,
    b_hidden,
    w_out,
    b_out,
    targets,
    var_weight,
    area_weight,
    edge_src,
    edge_coef,
    send_rows,
):
    mesh_rows, members, width = latent.shape
    shards = lax.axis_size("space")
    slots = send_rows.shape[2]
    variables, points = targets.shape
    points_all = points * shards
    own_rows = width // shards
    per_pair = slots * members
    rows = mesh_rows + shards * slots
    loss_columns = round_up(2 * shards, own_rows) // own_rows
    var_pad = round_up(variables + loss_columns, LANES)
    half_width = width // 2
    shape = jax.ShapeDtypeStruct
    me = lax.axis_index("space").astype(jnp.int32).reshape(1)

    latent_rows = latent.reshape(mesh_rows * members, width)
    slot_rows = jnp.swapaxes(send_rows, 1, 2)
    area_row = area_weight.reshape(1, points)
    outgoing = call(
        pack_kernel,
        shape((shards, slots, members, width + LANES), bf16),
        [SMEM, ANY, VMEM],
        [pltpu.VMEM((members, width), bf16), pltpu.SemaphoreType.DMA],
        1 << 24,
        slot_rows,
        latent,
        area_row,
        limit=PACK * MIB,
    )
    arrived = lax.all_to_all(outgoing, "space", split_axis=0, concat_axis=0, tiled=True)
    arrived = arrived.reshape(shards, per_pair, width + LANES)

    columns = (half_width + var_pad, half_width)
    layout = Layout(members, rows, points, var_pad, width)
    prepared, w_src_t = call(
        functools.partial(local_kernel, layout=layout, rows=rows),
        [shape(layout.shape, bf16), shape((width, width), bf16)],
        [VMEM] * 10,
        [
            pltpu.VMEM((width // LANES, mesh_rows * members, LANES), f32),
            pltpu.VMEM((var_pad, width), f32),
            pltpu.VMEM((var_pad, points), f32),
        ],
        1 << 31,
        latent_rows,
        w_src,
        edge_src.T,
        edge_coef.T,
        b_hidden.reshape(1, width),
        w_out.T,
        b_out.reshape(variables, 1),
        targets,
        var_weight.reshape(variables, 1),
        area_row,
        limit=56 * MIB,
    )

    operands = (w_src, prepared, latent_rows)
    dlocal, slot_grad, *pieces = call(
        functools.partial(
            decoder_kernel, layout=layout, points_all=points_all, variables=variables
        ),
        [
            shape((mesh_rows * members, width), bf16),
            shape((shards, per_pair, width), bf16),
            *[shape((shards // 2, own_rows, n), bf16) for n in columns for _ in range(2)],
        ],
        [SMEM, VMEM] + [HBM] * len(operands),
        [
            *[pltpu.VMEM(x.shape, x.dtype) for x in operands],
            pltpu.VMEM((members * points, width), bf16),
            pltpu.VMEM((members * points, width), bf16),
            pltpu.VMEM((2, points, width), f32),
            pltpu.VMEM((members, points, var_pad), f32),
            pltpu.VMEM((members, points, var_pad), bf16),
            pltpu.VMEM((points, var_pad), f32),
            pltpu.VMEM((points, var_pad), f32),
            pltpu.VMEM((width, var_pad), bf16),
            pltpu.VMEM((width // LANES, rows * members, LANES), f32),
            pltpu.VMEM((mesh_rows * members, width), bf16),
            pltpu.VMEM((shards, per_pair, width), bf16),
            pltpu.SemaphoreType.DMA((3,)),
        ],
        1 << 34,
        me,
        arrived,
        *operands,
        out_specs=[HBM] * 2 + [VMEM] * 4,
        limit=KEEP * MIB,
    )

    returned = lax.all_to_all(slot_grad, "space", split_axis=0, concat_axis=0, tiled=True)

    levels = [1 << i for i in reversed(range(1, shards.bit_length() - 1))]
    order_a = levels[::-1]
    order_b = order_a[1:2] + order_a[:1] + order_a[2:]
    left = [list(levels), list(levels)]
    count = shards // 2
    got = [swap(pieces[1], 1, shards), swap(pieces[3], 1, shards)]
    for step, bits in enumerate(zip(order_a, order_b, strict=True)):
        views = []
        for i, bit in enumerate(bits):
            place = left[i].index(bit)
            left[i].remove(bit)
            split = (1 << place, 2, count >> (place + 1), own_rows, columns[i])
            views += [pieces[2 * i].reshape(split), got[i].reshape(split)]
        count //= 2
        halves = [(x.shape[0], *x.shape[2:]) for x in views[::2] for _ in range(2)]
        pieces = call(
            functools.partial(halve_kernel, bits=bits),
            [shape(x, bf16) for x in halves],
            [SMEM] + [VMEM] * len(views),
            [],
            1 << 24,
            me,
            *views,
        )
        pieces = [x.reshape(count, *x.shape[2:]) for x in pieces]
        got = [swap(pieces[2 * i + 1], bit, shards) for i, bit in enumerate(bits)]

    grad_latent = call(
        latent_grad_kernel,
        shape((mesh_rows * members, width), f32),
        [SMEM, VMEM, HBM, HBM, ANY],
        [
            pltpu.VMEM((shards * per_pair, mesh_rows * members), f32),
            pltpu.VMEM((mesh_rows * members, width), bf16),
            pltpu.VMEM((width, width), bf16),
            pltpu.VMEM((mesh_rows * members, width), f32),
            pltpu.SemaphoreType.DMA((6,)),
        ],
        1 << 32,
        slot_rows,
        returned,
        dlocal,
        w_src_t,
        pieces[0],
        out_specs=[HBM],
        limit=56 * MIB,
    )
    grad_w_src, grad_w_out, loss = call(
        functools.partial(final_kernel, scale=WSCALE / points_all),
        [
            shape((own_rows, width), f32),
            shape((own_rows, variables), f32),
            shape((1, 1), f32),
        ],
        [VMEM] * 4,
        [],
        1 << 24,
        pieces[0],
        got[0],
        pieces[2],
        got[1],
    )
    return (
        loss.reshape(1),
        grad_latent.reshape(mesh_rows, members, width),
        grad_w_src,
        grad_w_out,
    )


def solution(mesh):
    placed = (
        P(("groups", "space"), None, None),
        P(),
        P(),
        P(),
        P(),
        P(None, ("groups", "space")),
        P(),
        P("space"),
        P("space", None),
        P("space", None),
        P("space", None, None),
    )
    return jax.shard_map(
        per_device,
        mesh=mesh,
        in_specs=placed,
        out_specs=(
            P("groups"),
            P(("groups", "space"), None, None),
            P(("groups", "space"), None),
            P(("groups", "space"), None),
        ),
        check_vma=False,
    )
```

```python
import functools
import math

import jax
import jax.numpy as jnp
from jax import lax
from jax.experimental import pallas as pl
from jax.experimental.pallas import tpu as pltpu
from jax.sharding import PartitionSpec as P

WSCALE = 2048
LANES = 128
ROWS = 16
alpha_fair = 0.95
smooth_sq = 0.01
MIB = 1 << 20
KEEP = 50
PACK = 56
UNROLL = 2
LAST = 54

f32 = jnp.float32
bf16 = jnp.bfloat16
NN = (((1,), (0,)), ((), ()))
TN = (((0,), (0,)), ((), ()))
NT = (((1,), (1,)), ((), ()))
SMEM = pl.BlockSpec(memory_space=pltpu.SMEM)
VMEM = pl.BlockSpec(memory_space=pltpu.VMEM)
ANY = pl.BlockSpec(memory_space=pl.ANY)
HBM = pl.BlockSpec(memory_space=pltpu.HBM)


def spread_coef(members):
    return alpha_fair / (2.0 * members * (members - 1)) + (1.0 - alpha_fair) / (
        2.0 * members * members
    )


def mm(a, b, dims=NN):
    return lax.dot_general(a, b, dims, preferred_element_type=f32)


def round_up(value, multiple):
    return -(-value // multiple) * multiple


def split_sum(value):
    high = value.astype(bf16)
    rest = value - high.astype(f32)
    middle = rest.astype(bf16)
    return high, middle, (rest - middle.astype(f32)).astype(bf16)


def project(projected, rows, w_src):
    out = mm(rows, w_src[...])
    for c in range(projected.shape[0]):
        projected[c, : rows.shape[0], :] = out[:, c * LANES : (c + 1) * LANES]


def by_member(projected, table, members, rows_pad, first, count):
    for m in range(members):
        at = m * rows_pad + first
        for c in range(projected.shape[0]):
            block = projected[c, pl.ds(m, count, stride=members), :]
            table[at : at + count, c * LANES : (c + 1) * LANES] = block.astype(bf16)


def pack_kernel(rows_ref, latent, area, out, zeros, sem):
    shards, slots, members, _ = out.shape
    width = zeros.shape[1]
    zeros[...] = jnp.zeros_like(zeros)
    for s in range(shards):
        for b in range(slots):
            row = rows_ref[0, b, s]
            target = out.at[s, b, :, pl.ds(0, width)]

            @pl.when(row >= 0)
            def _(row=row, target=target):
                pltpu.make_async_copy(latent.at[row], target, sem).start()

            @pl.when(row < 0)
            def _(target=target):
                pltpu.make_async_copy(zeros, target, sem).start()

    total = jnp.sum(area[...], axis=1, keepdims=True) + jnp.zeros((members, LANES), f32)
    lane = lax.broadcasted_iota(jnp.int32, (members, LANES), 1)
    tail = jnp.zeros((members, LANES), f32)
    for i, piece in enumerate(split_sum(total)):
        tail = jnp.where(lane == i, piece.astype(f32), tail)
    tail = tail.astype(bf16)
    for s in range(shards):
        for b in range(slots):
            out[s, b, :, width:] = tail
    for s in range(shards):
        for b in range(slots):
            pltpu.make_async_copy(zeros, out.at[s, b, :, pl.ds(0, width)], sem).wait()


def strips(widths, width):
    places, strip, first = [], 0, 0
    for w in widths:
        if first + w > width:
            strip, first = strip + 1, 0
        places.append((strip, first))
        first += w
    return places, strip + 1


class Layout:
    def __init__(self, members, rows, points, var_pad, width):
        self.rows_pad = round_up(rows + 2, ROWS)
        self.out_first = members * self.rows_pad
        self.point_first = self.out_first + var_pad
        widths = [var_pad] * 6 + [round_up(self.rows_pad, LANES)]
        self.places, count = strips(widths, width)
        self.points = points
        self.edge_first = self.point_first + count * points
        self.shape = (self.edge_first + rows, width)

    def point_block(self, ref, i, columns):
        strip, first = self.places[i]
        at = self.point_first + strip * self.points
        return ref.at[pl.ds(at, self.points), pl.ds(first, columns)]


def local_kernel(
    latent,
    w_src,
    edge_src,
    edge_coef,
    b_hidden,
    w_out_t,
    b_out,
    targets,
    var_weight,
    area_weight,
    prepared,
    w_src_t,
    projected,
    wide,
    tall,
    *,
    layout,
    rows,
):
    variables, width = w_out_t.shape
    points = edge_src.shape[1]
    rows_pad = layout.rows_pad
    members = layout.out_first // rows_pad
    mesh_rows = latent.shape[0] // members
    var_pad = wide.shape[0]
    project(projected, latent[...], w_src)
    by_member(projected, prepared, members, rows_pad, 0, mesh_rows)

    row = lax.broadcasted_iota(jnp.int32, (rows_pad, points), 0)
    matrix = jnp.where((row >= rows) & (row < rows + 2), 0.5, 0.0).astype(f32)
    for k in range(edge_src.shape[0]):
        matrix = matrix + jnp.where(
            row == edge_src[k : k + 1, :], 0.5 * edge_coef[k : k + 1, :], 0.0
        )
    prepared[layout.edge_first :, :points] = matrix[:rows].astype(bf16)
    layout.point_block(prepared, 6, rows_pad)[...] = matrix.T.astype(bf16)

    high, low, _ = split_sum(b_hidden[...])
    at = lax.broadcasted_iota(jnp.int32, (rows_pad - rows, width), 0)
    bias_rows = jnp.where(
        at == 0, high.astype(f32), jnp.where(at == 1, low.astype(f32), 0.0)
    ).astype(bf16)
    for m in range(members):
        prepared[m * rows_pad + rows : (m + 1) * rows_pad, :] = bias_rows

    wide[...] = jnp.zeros_like(wide)
    wide[:variables, :] = w_out_t[...].astype(f32)
    prepared[layout.out_first : layout.point_first, :] = wide[...].astype(bf16)

    for i, value in ((0, targets[...] - b_out[...]), (3, var_weight[...] * area_weight[...])):
        tall[...] = jnp.zeros_like(tall)
        tall[:variables, :] = value
        for j, piece in enumerate(split_sum(tall[...].T)):
            layout.point_block(prepared, i + j, var_pad)[...] = piece
    w_src_t[...] = w_src[...].T


def decoder_kernel(
    me_ref,
    arrived,
    w_src_hbm,
    prepared_hbm,
    latent_hbm,
    dlocal_hbm,
    slot_grad_hbm,
    keep_a,
    send_a,
    keep_b,
    send_b,
    w_src,
    prepared,
    latent,
    hidden,
    slope,
    preact,
    dpreact,
    pred,
    dpred,
    truth,
    weighting,
    w_out_pad,
    dtable,
    dlocal,
    slot_grad,
    sem,
    *,
    layout,
    points_all,
    variables,
):
    shards, per_pair, _ = arrived.shape
    received = shards * per_pair
    own, width = latent.shape
    members, points, var_pad = pred.shape
    mesh_rows = own // members
    rows = mesh_rows + received // members
    rows_pad = layout.rows_pad
    me = me_ref[0]

    loads = [
        pltpu.make_async_copy(source, target, sem.at[i])
        for i, (source, target) in enumerate(
            ((w_src_hbm, w_src), (prepared_hbm, prepared), (latent_hbm, latent))
        )
    ]
    for load in loads:
        load.start()

    loads[0].wait()
    arrived_rows = arrived[:, :, :width].reshape(received, width)
    project(dtable, arrived_rows, w_src)
    loads[1].wait()
    by_member(dtable, prepared, members, rows_pad, mesh_rows, received // members)
    w_out_t_pad = prepared[layout.out_first : layout.point_first, :]
    w_out_pad[...] = w_out_t_pad.T
    for i, target in ((0, truth), (3, weighting)):
        target[...] = sum(
            layout.point_block(prepared, i + j, var_pad)[...].astype(f32) for j in range(3)
        )

    tail = arrived[:, :, width:].astype(f32)
    at_row = lax.broadcasted_iota(jnp.int32, tail.shape, 1)
    at_lane = lax.broadcasted_iota(jnp.int32, tail.shape, 2)
    tail = jnp.where((at_row == 0) & (at_lane < 3), tail, 0.0)
    mean_area = jnp.sum(jnp.sum(tail, axis=0), keepdims=True) / points_all

    c0 = math.sqrt(2.0 / math.pi)
    c1 = c0 * 0.044715
    quarter = width // 4

    def gather(m, slot, c):
        left, right = c * quarter, (c + 1) * quarter
        table = prepared[m * rows_pad : (m + 1) * rows_pad, left:right]
        preact[slot, :, left:right] = mm(layout.point_block(prepared, 6, rows_pad)[...], table)

    for c in range(4):
        gather(0, 0, c)

    for m in range(members):
        slot = m % 2
        first = m * points
        for c in range(4):
            left, right = c * quarter, (c + 1) * quarter
            if m + 1 < members:
                gather(m + 1, 1 - slot, c)
            for r in range(0, points, ROWS):
                y = preact[slot, r : r + ROWS, left:right]
                y2 = y * y
                t = jnp.tanh(y * (2.0 * c0 + (8.0 * c1) * y2))
                p = 1.0 + t
                gelu = y * p
                hidden[first + r : first + r + ROWS, left:right] = gelu.astype(bf16)
                bend = (gelu * (1.0 - t)) * (2.0 * c0 + (24.0 * c1) * y2)
                slope[first + r : first + r + ROWS, left:right] = (p + bend).astype(bf16)
        pred[m] = mm(hidden[first : first + points, :], w_out_pad[...])

    spread = spread_coef(members)
    inverse_mean = 1.0 / mean_area
    loss_sum = jnp.zeros((ROWS, LANES), f32)
    for left in range(0, var_pad, LANES):

        def score(block, loss_sum, left=left):
            at = pl.ds(pl.multiple_of(block * ROWS, ROWS), ROWS)
            p = [pred[m, at, left : left + LANES] for m in range(members)]
            true = truth[at, left : left + LANES]
            weight = weighting[at, left : left + LANES]
            fit = jnp.zeros((ROWS, LANES), f32)
            grads = []
            for m in range(members):
                d = p[m] - true
                q = d * d + smooth_sq
                r = lax.rsqrt(q)
                fit = fit + q * r
                grads.append(d * r * (1.0 / members))
            pairs = jnp.zeros((ROWS, LANES), f32)
            apart = [jnp.zeros((ROWS, LANES), f32) for _ in range(members)]
            for j in range(members):
                for k in range(j + 1, members):
                    d = p[j] - p[k]
                    q = d * d + smooth_sq
                    r = lax.rsqrt(q)
                    pairs = pairs + q * r
                    s = d * r
                    apart[j] = apart[j] + s
                    apart[k] = apart[k] - s
            scaled = weight * inverse_mean
            for m in range(members):
                gradient = grads[m] - (2.0 * spread) * apart[m]
                dpred[m, at, left : left + LANES] = (gradient * scaled).astype(bf16)
            return loss_sum + weight * (fit * (1.0 / members) - (2.0 * spread) * pairs)

        loss_sum = lax.fori_loop(0, points // ROWS, score, loss_sum, unroll=UNROLL)
    loss = jnp.sum(loss_sum, keepdims=True) * (inverse_mean / points_all)

    edge_back = prepared[layout.edge_first :, :points]
    preact[0] = mm(dpred[0], w_out_t_pad)
    for m in range(members + 1):
        if m + 1 < members:
            preact[(m + 1) % 2] = mm(dpred[m + 1], w_out_t_pad)
        if m < members:
            for r in range(0, points, ROWS):
                at = m * points + r
                grad = preact[m % 2, r : r + ROWS, :] * slope[at : at + ROWS, :].astype(f32)
                dpreact[m % 2, r : r + ROWS, :] = grad.astype(bf16)
        if m >= 1:
            grad = mm(edge_back, dpreact[(m - 1) % 2])
            for c in range(width // LANES):
                dtable[c, pl.ds(m - 1, rows, stride=members), :] = grad[
                    :, c * LANES : (c + 1) * LANES
                ]

    for c in range(width // LANES):
        left, right = c * LANES, (c + 1) * LANES
        dlocal[:, left:right] = dtable[c, :own, :].astype(bf16)
        slot_grad[:, :, left:right] = (
            dtable[c, own:, :].astype(bf16).reshape(shards, per_pair, LANES)
        )
    stores = [
        pltpu.make_async_copy(slot_grad, slot_grad_hbm, sem.at[0]),
        pltpu.make_async_copy(dlocal, dlocal_hbm, sem.at[1]),
    ]
    for store in stores:
        store.start()

    half_width = width // 2
    pairs, own_rows, _ = keep_a.shape
    core = lax.rem(me, 2)
    grad = mm(dpred[...].reshape(members * points, var_pad), hidden[...], TN).T
    row = lax.broadcasted_iota(jnp.int32, grad.shape, 0)
    lane = lax.broadcasted_iota(jnp.int32, grad.shape, 1)
    row = row & (own_rows - 1)
    grad = jnp.where(lane < variables, grad, 0.0)
    for i, piece in enumerate(split_sum(loss)[:2]):
        place = me * 2 + i
        here = (row == lax.rem(place, own_rows)) & (lane == variables + place // own_rows)
        grad = jnp.where(here, piece.astype(f32), grad)
    grad = grad.astype(bf16).reshape(pairs, 2, own_rows, var_pad)
    keep_a[:, :, half_width:] = jnp.where(core == 0, grad[:, 0], grad[:, 1])
    send_a[:, :, half_width:] = jnp.where(core == 0, grad[:, 1], grad[:, 0])
    loads[2].wait()
    back = slot_grad[...].reshape(received, width)
    for left, keep, send in ((0, keep_a, send_a), (half_width, keep_b, send_b)):
        right = left + half_width
        grad = mm(latent[...], dlocal[:, left:right], TN)
        grad = grad + mm(arrived_rows, back[:, left:right], TN)
        grad = grad.astype(bf16).reshape(pairs, 2, own_rows, half_width)
        keep[:, :, :half_width] = jnp.where(core == 0, grad[:, 0], grad[:, 1])
        send[:, :, :half_width] = jnp.where(core == 0, grad[:, 1], grad[:, 0])
    for store in stores:
        store.wait()


def halve_kernel(me_ref, *refs, parts):
    outs = refs[2 * len(parts) :]
    for i, (bit, (first, last), place, (left, right)) in enumerate(parts):
        keep, got = refs[2 * i], refs[2 * i + 1]
        mine = lax.rem(me_ref[0] // bit, 2)
        for out, half in ((outs[2 * place + 1], 1 - mine), (outs[2 * place], mine)):
            total = keep[:, half, :, :, first:last].astype(f32)
            total = total + got[:, half, :, :, first:last].astype(f32)
            out[:, :, :, left:right] = total.astype(bf16)


def final_kernel(keep, got, grad_w_src, grad_w_out, loss, *, scale):
    variables = grad_w_out.shape[1]
    half_width = grad_w_src.shape[1] // 2
    second = keep.shape[2] - half_width
    total = keep[0].astype(f32) + got[0].astype(f32)
    grad_w_src[:, :half_width] = total[:, :half_width] * scale
    grad_w_src[:, half_width:] = total[:, second:] * scale
    out = total[:, half_width:second]
    grad_w_out[...] = out[:, :variables] * scale
    lane = lax.broadcasted_iota(jnp.int32, out.shape, 1)
    loss[...] = jnp.sum(jnp.where(lane >= variables, out, 0.0), keepdims=True)


def latent_grad_kernel(
    rows_ref, returned, dlocal_hbm, w_src_t_hbm, _, out_hbm, selector, dlocal, w_src_t, out, sem
):
    shards, per_pair, width = returned.shape
    _, slots, _ = rows_ref.shape
    members = per_pair // slots
    loads = [
        pltpu.make_async_copy(w_src_t_hbm, w_src_t, sem.at[0]),
        pltpu.make_async_copy(dlocal_hbm, dlocal, sem.at[1]),
    ]
    for load in loads:
        load.start()
    lane = lax.broadcasted_iota(jnp.int32, (members, selector.shape[1]), 1)
    member = lax.broadcasted_iota(jnp.int32, (members, selector.shape[1]), 0)
    for s in range(shards):
        for b in range(slots):
            first = (s * slots + b) * members
            selector[first : first + members, :] = jnp.where(
                lane == rows_ref[0, b, s] * members + member, 1.0, 0.0
            ).astype(f32)
    back = returned[...].reshape(shards * per_pair, width)
    spread = mm(selector[...].astype(bf16), back, TN)
    for load in loads:
        load.wait()
    total = (dlocal[...].astype(f32) + spread).astype(bf16)
    stores = []
    chunk = width // 4
    for i in range(4):
        part = pl.ds(i * chunk, chunk)
        out[:, part] = mm(total, w_src_t[:, part])
        stores.append(
            pltpu.make_async_copy(out.at[:, part], out_hbm.at[:, part], sem.at[2 + i])
        )
        stores[-1].start()
    for store in stores:
        store.wait()


def size_of(x):
    return math.prod(x.shape) * jnp.dtype(x.dtype).itemsize


def call(kernel, out_shape, in_specs, scratch, cost, *args, out_specs=None, limit=None):
    single = not isinstance(out_shape, (list, tuple))
    outs = [out_shape] if single else list(out_shape)
    specs = out_specs or [VMEM] * len(outs)
    used = sum(size_of(x) for x, s in zip(args, in_specs, strict=True) if s is VMEM)
    used += sum(size_of(x) for x, s in zip(outs, specs, strict=True) if s is VMEM)
    used += sum(size_of(x) for x in scratch if getattr(x, "dtype", None) in (f32, bf16))
    limit = limit or used + used // 4 + 6 * MIB
    if used > limit * 4 // 5:
        limit = 60 * MIB
    return pl.pallas_call(
        kernel,
        out_shape=out_shape,
        in_specs=in_specs,
        out_specs=specs[0] if single else specs,
        scratch_shapes=scratch,
        compiler_params=pltpu.CompilerParams(vmem_limit_bytes=limit),
        cost_estimate=pl.CostEstimate(flops=cost, bytes_accessed=used, transcendentals=0),
    )(*args)


def swap(value, bit, shards):
    return lax.ppermute(value, "space", [(i, i ^ bit) for i in range(shards)])


def per_device(
    latent,
    w_src,
    b_hidden,
    w_out,
    b_out,
    targets,
    var_weight,
    area_weight,
    edge_src,
    edge_coef,
    send_rows,
):
    mesh_rows, members, width = latent.shape
    shards = lax.axis_size("space")
    slots = send_rows.shape[2]
    variables, points = targets.shape
    points_all = points * shards
    own_rows = width // shards
    per_pair = slots * members
    rows = mesh_rows + shards * slots
    loss_columns = round_up(2 * shards, own_rows) // own_rows
    var_pad = round_up(variables + loss_columns, LANES)
    half_width = width // 2
    shape = jax.ShapeDtypeStruct
    me = lax.axis_index("space").astype(jnp.int32).reshape(1)

    latent_rows = latent.reshape(mesh_rows * members, width)
    slot_rows = jnp.swapaxes(send_rows, 1, 2)
    area_row = area_weight.reshape(1, points)
    outgoing = call(
        pack_kernel,
        shape((shards, slots, members, width + LANES), bf16),
        [SMEM, ANY, VMEM],
        [pltpu.VMEM((members, width), bf16), pltpu.SemaphoreType.DMA],
        1 << 24,
        slot_rows,
        latent,
        area_row,
        limit=PACK * MIB,
    )
    arrived = lax.all_to_all(outgoing, "space", split_axis=0, concat_axis=0, tiled=True)
    arrived = arrived.reshape(shards, per_pair, width + LANES)

    columns = width + var_pad
    cut = half_width + var_pad
    layout = Layout(members, rows, points, var_pad, width)
    prepared, w_src_t = call(
        functools.partial(local_kernel, layout=layout, rows=rows),
        [shape(layout.shape, bf16), shape((width, width), bf16)],
        [VMEM] * 10,
        [
            pltpu.VMEM((width // LANES, mesh_rows * members, LANES), f32),
            pltpu.VMEM((var_pad, width), f32),
            pltpu.VMEM((var_pad, points), f32),
        ],
        1 << 31,
        latent_rows,
        w_src,
        edge_src.T,
        edge_coef.T,
        b_hidden.reshape(1, width),
        w_out.T,
        b_out.reshape(variables, 1),
        targets,
        var_weight.reshape(variables, 1),
        area_row,
        limit=56 * MIB,
    )

    operands = (w_src, prepared, latent_rows)
    dlocal, slot_grad, *pieces = call(
        functools.partial(
            decoder_kernel, layout=layout, points_all=points_all, variables=variables
        ),
        [
            shape((mesh_rows * members, width), bf16),
            shape((shards, per_pair, width), bf16),
            *[shape((shards // 2, own_rows, n), bf16) for n in (cut, half_width) for _ in range(2)],
        ],
        [SMEM, VMEM] + [HBM] * len(operands),
        [
            *[pltpu.VMEM(x.shape, x.dtype) for x in operands],
            pltpu.VMEM((members * points, width), bf16),
            pltpu.VMEM((members * points, width), bf16),
            pltpu.VMEM((2, points, width), f32),
            pltpu.VMEM((2, points, width), bf16),
            pltpu.VMEM((members, points, var_pad), f32),
            pltpu.VMEM((members, points, var_pad), bf16),
            pltpu.VMEM((points, var_pad), f32),
            pltpu.VMEM((points, var_pad), f32),
            pltpu.VMEM((width, var_pad), bf16),
            pltpu.VMEM((width // LANES, rows * members, LANES), f32),
            pltpu.VMEM((mesh_rows * members, width), bf16),
            pltpu.VMEM((shards, per_pair, width), bf16),
            pltpu.SemaphoreType.DMA((3,)),
        ],
        1 << 34,
        me,
        arrived,
        *operands,
        out_specs=[HBM] * 2 + [VMEM] * 4,
        limit=KEEP * MIB,
    )

    returned = lax.all_to_all(slot_grad, "space", split_axis=0, concat_axis=0, tiled=True)

    levels = [1 << i for i in reversed(range(1, shards.bit_length() - 1))]
    order_a = levels[::-1]
    order_b = order_a[1:2] + order_a[:1] + order_a[2:]
    left = [list(levels), list(levels)]
    held = [(pieces[i], swap(pieces[i + 1], 1, shards)) for i in (0, 2)]
    count = shards // 2
    for step, bits in enumerate(zip(order_a, order_b, strict=True)):
        views, parts = [], []
        for i, bit in enumerate(bits):
            place = left[i].index(bit)
            left[i].remove(bit)
            if step > 2 and i == 1:
                break
            pair = held[i]
            split = (1 << place, 2, count >> (place + 1), own_rows)
            views += [x.reshape(*split, x.shape[2]) for x in pair]
            mine = (0, cut) if i == 0 else (cut, columns)
            alone = (0, mine[1] - mine[0])
            if step < 2:
                parts.append((bit, alone, i, alone))
            elif step == 2:
                parts.append((bit, alone, 0, mine))
            else:
                parts.append((bit, (0, columns), 0, (0, columns)))
        widths = (cut, columns - cut) if step < 2 else (columns,)
        count //= 2
        outs = []
        for i, w in enumerate(widths):
            hi, _, lo = views[2 * i].shape[:3]
            outs += [shape((hi, lo, own_rows, w), bf16)] * 2
        pieces = call(
            functools.partial(halve_kernel, parts=tuple(parts)),
            outs,
            [SMEM] + [VMEM] * len(views),
            [],
            1 << 24,
            me,
            *views,
        )
        pieces = [x.reshape(count, own_rows, x.shape[3]) for x in pieces]
        held = [
            (pieces[2 * i], swap(pieces[2 * i + 1], bits[i], shards)) for i in range(len(widths))
        ]

    grad_latent = call(
        latent_grad_kernel,
        shape((mesh_rows * members, width), f32),
        [SMEM, VMEM, HBM, HBM, ANY],
        [
            pltpu.VMEM((shards * per_pair, mesh_rows * members), f32),
            pltpu.VMEM((mesh_rows * members, width), bf16),
            pltpu.VMEM((width, width), bf16),
            pltpu.VMEM((mesh_rows * members, width), f32),
            pltpu.SemaphoreType.DMA((6,)),
        ],
        1 << 32,
        slot_rows,
        returned,
        dlocal,
        w_src_t,
        held[0][0],
        out_specs=[HBM],
        limit=LAST * MIB,
    )
    grad_w_src, grad_w_out, loss = call(
        functools.partial(final_kernel, scale=WSCALE / points_all),
        [
            shape((own_rows, width), f32),
            shape((own_rows, variables), f32),
            shape((1, 1), f32),
        ],
        [VMEM] * 2,
        [],
        1 << 24,
        *held[0],
    )
    return (
        loss.reshape(1),
        grad_latent.reshape(mesh_rows, members, width),
        grad_w_src,
        grad_w_out,
    )


def solution(mesh):
    placed = (
        P(("groups", "space"), None, None),
        P(),
        P(),
        P(),
        P(),
        P(None, ("groups", "space")),
        P(),
        P("space"),
        P("space", None),
        P("space", None),
        P("space", None, None),
    )
    return jax.shard_map(
        per_device,
        mesh=mesh,
        in_specs=placed,
        out_specs=(
            P("groups"),
            P(("groups", "space"), None, None),
            P(("groups", "space"), None),
            P(("groups", "space"), None),
        ),
        check_vma=False,
    )
```

```python
import functools
import math

import jax
import jax.numpy as jnp
from jax import lax
from jax.experimental import pallas as pl
from jax.experimental.pallas import tpu as pltpu
from jax.sharding import PartitionSpec as P

WSCALE = 2048
LANES = 128
ROWS = 16
alpha_fair = 0.95
smooth_sq = 0.01
MIB = 1 << 20
KEEP = 50
PACK = 56
UNROLL = 2
LAST = 54

f32 = jnp.float32
bf16 = jnp.bfloat16
NN = (((1,), (0,)), ((), ()))
TN = (((0,), (0,)), ((), ()))
NT = (((1,), (1,)), ((), ()))
SMEM = pl.BlockSpec(memory_space=pltpu.SMEM)
VMEM = pl.BlockSpec(memory_space=pltpu.VMEM)
ANY = pl.BlockSpec(memory_space=pl.ANY)
HBM = pl.BlockSpec(memory_space=pltpu.HBM)


def spread_coef(members):
    return alpha_fair / (2.0 * members * (members - 1)) + (1.0 - alpha_fair) / (
        2.0 * members * members
    )


def mm(a, b, dims=NN):
    return lax.dot_general(a, b, dims, preferred_element_type=f32)


def round_up(value, multiple):
    return -(-value // multiple) * multiple


def split_sum(value):
    high = value.astype(bf16)
    rest = value - high.astype(f32)
    middle = rest.astype(bf16)
    return high, middle, (rest - middle.astype(f32)).astype(bf16)


def project(projected, rows, w_src):
    out = mm(rows, w_src[...])
    for c in range(projected.shape[0]):
        projected[c, : rows.shape[0], :] = out[:, c * LANES : (c + 1) * LANES]


def by_member(projected, table, members, rows_pad, first, count):
    for m in range(members):
        at = m * rows_pad + first
        for c in range(projected.shape[0]):
            block = projected[c, pl.ds(m, count, stride=members), :]
            table[at : at + count, c * LANES : (c + 1) * LANES] = block.astype(bf16)


def fill_selector(selector, rows_ref, members):
    _, slots, shards = rows_ref.shape
    lane = lax.broadcasted_iota(jnp.int32, (members, selector.shape[1]), 1)
    member = lax.broadcasted_iota(jnp.int32, (members, selector.shape[1]), 0)
    for s in range(shards):
        for b in range(slots):
            first = (s * slots + b) * members
            selector[first : first + members, :] = jnp.where(
                lane == rows_ref[0, b, s] * members + member, 1.0, 0.0
            ).astype(f32)


def pack_kernel(rows_ref, latent, area, out, selector, *, members):
    shards, per_pair, _ = out.shape
    width = latent.shape[1]
    fill_selector(selector, rows_ref, members)
    picked = mm(selector[...].astype(bf16), latent[...])
    out[:, :, :width] = picked.astype(bf16).reshape(shards, per_pair, width)
    total = jnp.sum(area[...], axis=1, keepdims=True) + jnp.zeros((per_pair, LANES), f32)
    lane = lax.broadcasted_iota(jnp.int32, (per_pair, LANES), 1)
    tail = jnp.zeros((per_pair, LANES), f32)
    for i, piece in enumerate(split_sum(total)):
        tail = jnp.where(lane == i, piece.astype(f32), tail)
    tail = tail.astype(bf16)
    for s in range(shards):
        out[s, :, width:] = tail


def strips(widths, width):
    places, strip, first = [], 0, 0
    for w in widths:
        if first + w > width:
            strip, first = strip + 1, 0
        places.append((strip, first))
        first += w
    return places, strip + 1


class Layout:
    def __init__(self, members, rows, points, var_pad, width):
        self.rows_pad = round_up(rows + 2, ROWS)
        self.out_first = members * self.rows_pad
        self.point_first = self.out_first + var_pad
        widths = [var_pad] * 6 + [round_up(self.rows_pad, LANES)]
        self.places, count = strips(widths, width)
        self.points = points
        self.edge_first = self.point_first + count * points
        self.shape = (self.edge_first + rows, width)

    def point_block(self, ref, i, columns):
        strip, first = self.places[i]
        at = self.point_first + strip * self.points
        return ref.at[pl.ds(at, self.points), pl.ds(first, columns)]


def local_kernel(
    latent,
    w_src,
    edge_src,
    edge_coef,
    b_hidden,
    w_out_t,
    b_out,
    targets,
    var_weight,
    area_weight,
    prepared,
    w_src_t,
    projected,
    wide,
    tall,
    *,
    layout,
    rows,
):
    variables, width = w_out_t.shape
    points = edge_src.shape[1]
    rows_pad = layout.rows_pad
    members = layout.out_first // rows_pad
    mesh_rows = latent.shape[0] // members
    var_pad = wide.shape[0]
    project(projected, latent[...], w_src)
    by_member(projected, prepared, members, rows_pad, 0, mesh_rows)

    row = lax.broadcasted_iota(jnp.int32, (rows_pad, points), 0)
    matrix = jnp.where((row >= rows) & (row < rows + 2), 0.5, 0.0).astype(f32)
    for k in range(edge_src.shape[0]):
        matrix = matrix + jnp.where(
            row == edge_src[k : k + 1, :], 0.5 * edge_coef[k : k + 1, :], 0.0
        )
    prepared[layout.edge_first :, :points] = matrix[:rows].astype(bf16)
    layout.point_block(prepared, 6, rows_pad)[...] = matrix.T.astype(bf16)

    high, low, _ = split_sum(b_hidden[...])
    at = lax.broadcasted_iota(jnp.int32, (rows_pad - rows, width), 0)
    bias_rows = jnp.where(
        at == 0, high.astype(f32), jnp.where(at == 1, low.astype(f32), 0.0)
    ).astype(bf16)
    for m in range(members):
        prepared[m * rows_pad + rows : (m + 1) * rows_pad, :] = bias_rows

    wide[...] = jnp.zeros_like(wide)
    wide[:variables, :] = w_out_t[...].astype(f32)
    prepared[layout.out_first : layout.point_first, :] = wide[...].astype(bf16)

    for i, value in ((0, targets[...] - b_out[...]), (3, var_weight[...] * area_weight[...])):
        tall[...] = jnp.zeros_like(tall)
        tall[:variables, :] = value
        for j, piece in enumerate(split_sum(tall[...].T)):
            layout.point_block(prepared, i + j, var_pad)[...] = piece
    w_src_t[...] = w_src[...].T


def decoder_kernel(
    me_ref,
    arrived,
    w_src_hbm,
    prepared_hbm,
    latent_hbm,
    dlocal_hbm,
    slot_grad_hbm,
    keep_a,
    send_a,
    keep_b,
    send_b,
    w_src,
    prepared,
    latent,
    hidden,
    slope,
    preact,
    dpreact,
    pred,
    dpred,
    truth,
    weighting,
    w_out_pad,
    dtable,
    dlocal,
    slot_grad,
    sem,
    *,
    layout,
    points_all,
    variables,
):
    shards, per_pair, _ = arrived.shape
    received = shards * per_pair
    own, width = latent.shape
    members, points, var_pad = pred.shape
    mesh_rows = own // members
    rows = mesh_rows + received // members
    rows_pad = layout.rows_pad
    me = me_ref[0]

    loads = [
        pltpu.make_async_copy(source, target, sem.at[i])
        for i, (source, target) in enumerate(
            ((w_src_hbm, w_src), (prepared_hbm, prepared), (latent_hbm, latent))
        )
    ]
    for load in loads:
        load.start()

    loads[0].wait()
    arrived_rows = arrived[:, :, :width].reshape(received, width)
    project(dtable, arrived_rows, w_src)
    loads[1].wait()
    by_member(dtable, prepared, members, rows_pad, mesh_rows, received // members)
    w_out_t_pad = prepared[layout.out_first : layout.point_first, :]
    w_out_pad[...] = w_out_t_pad.T
    for i, target in ((0, truth), (3, weighting)):
        target[...] = sum(
            layout.point_block(prepared, i + j, var_pad)[...].astype(f32) for j in range(3)
        )

    tail = arrived[:, :, width:].astype(f32)
    at_row = lax.broadcasted_iota(jnp.int32, tail.shape, 1)
    at_lane = lax.broadcasted_iota(jnp.int32, tail.shape, 2)
    tail = jnp.where((at_row == 0) & (at_lane < 3), tail, 0.0)
    mean_area = jnp.sum(jnp.sum(tail, axis=0), keepdims=True) / points_all

    c0 = math.sqrt(2.0 / math.pi)
    c1 = c0 * 0.044715
    quarter = width // 4

    def gather(m, slot, c):
        left, right = c * quarter, (c + 1) * quarter
        table = prepared[m * rows_pad : (m + 1) * rows_pad, left:right]
        preact[slot, :, left:right] = mm(layout.point_block(prepared, 6, rows_pad)[...], table)

    for c in range(4):
        gather(0, 0, c)

    for m in range(members):
        slot = m % 2
        first = m * points
        for c in range(4):
            left, right = c * quarter, (c + 1) * quarter
            if m + 1 < members:
                gather(m + 1, 1 - slot, c)
            for r in range(0, points, ROWS):
                y = preact[slot, r : r + ROWS, left:right]
                y2 = y * y
                t = jnp.tanh(y * (2.0 * c0 + (8.0 * c1) * y2))
                p = 1.0 + t
                gelu = y * p
                hidden[first + r : first + r + ROWS, left:right] = gelu.astype(bf16)
                bend = (gelu * (1.0 - t)) * (2.0 * c0 + (24.0 * c1) * y2)
                slope[first + r : first + r + ROWS, left:right] = (p + bend).astype(bf16)
        pred[m] = mm(hidden[first : first + points, :], w_out_pad[...])

    spread = spread_coef(members)
    inverse_mean = 1.0 / mean_area
    loss_sum = jnp.zeros((ROWS, LANES), f32)
    for left in range(0, var_pad, LANES):

        def score(block, loss_sum, left=left):
            at = pl.ds(pl.multiple_of(block * ROWS, ROWS), ROWS)
            p = [pred[m, at, left : left + LANES] for m in range(members)]
            true = truth[at, left : left + LANES]
            weight = weighting[at, left : left + LANES]
            fit = jnp.zeros((ROWS, LANES), f32)
            grads = []
            for m in range(members):
                d = p[m] - true
                q = d * d + smooth_sq
                r = lax.rsqrt(q)
                fit = fit + q * r
                grads.append(d * r * (1.0 / members))
            pairs = jnp.zeros((ROWS, LANES), f32)
            apart = [jnp.zeros((ROWS, LANES), f32) for _ in range(members)]
            for j in range(members):
                for k in range(j + 1, members):
                    d = p[j] - p[k]
                    q = d * d + smooth_sq
                    r = lax.rsqrt(q)
                    pairs = pairs + q * r
                    s = d * r
                    apart[j] = apart[j] + s
                    apart[k] = apart[k] - s
            scaled = weight * inverse_mean
            for m in range(members):
                gradient = grads[m] - (2.0 * spread) * apart[m]
                dpred[m, at, left : left + LANES] = (gradient * scaled).astype(bf16)
            return loss_sum + weight * (fit * (1.0 / members) - (2.0 * spread) * pairs)

        loss_sum = lax.fori_loop(0, points // ROWS, score, loss_sum, unroll=UNROLL)
    loss = jnp.sum(loss_sum, keepdims=True) * (inverse_mean / points_all)

    edge_back = prepared[layout.edge_first :, :points]
    preact[0] = mm(dpred[0], w_out_t_pad)
    for m in range(members + 1):
        if m + 1 < members:
            preact[(m + 1) % 2] = mm(dpred[m + 1], w_out_t_pad)
        if m < members:
            for r in range(0, points, ROWS):
                at = m * points + r
                grad = preact[m % 2, r : r + ROWS, :] * slope[at : at + ROWS, :].astype(f32)
                dpreact[m % 2, r : r + ROWS, :] = grad.astype(bf16)
        if m >= 1:
            grad = mm(edge_back, dpreact[(m - 1) % 2])
            for c in range(width // LANES):
                dtable[c, pl.ds(m - 1, rows, stride=members), :] = grad[
                    :, c * LANES : (c + 1) * LANES
                ]

    for c in range(width // LANES):
        left, right = c * LANES, (c + 1) * LANES
        dlocal[:, left:right] = dtable[c, :own, :].astype(bf16)
        slot_grad[:, :, left:right] = (
            dtable[c, own:, :].astype(bf16).reshape(shards, per_pair, LANES)
        )
    stores = [
        pltpu.make_async_copy(slot_grad, slot_grad_hbm, sem.at[0]),
        pltpu.make_async_copy(dlocal, dlocal_hbm, sem.at[1]),
    ]
    for store in stores:
        store.start()

    half_width = width // 2
    pairs, own_rows, _ = keep_a.shape
    core = lax.rem(me, 2)
    grad = mm(dpred[...].reshape(members * points, var_pad), hidden[...], TN).T
    row = lax.broadcasted_iota(jnp.int32, grad.shape, 0)
    lane = lax.broadcasted_iota(jnp.int32, grad.shape, 1)
    row = row & (own_rows - 1)
    grad = jnp.where(lane < variables, grad, 0.0)
    for i, piece in enumerate(split_sum(loss)[:2]):
        place = me * 2 + i
        here = (row == lax.rem(place, own_rows)) & (lane == variables + place // own_rows)
        grad = jnp.where(here, piece.astype(f32), grad)
    grad = grad.astype(bf16).reshape(pairs, 2, own_rows, var_pad)
    keep_a[:, :, half_width:] = jnp.where(core == 0, grad[:, 0], grad[:, 1])
    send_a[:, :, half_width:] = jnp.where(core == 0, grad[:, 1], grad[:, 0])
    loads[2].wait()
    back = slot_grad[...].reshape(received, width)
    for left, keep, send in ((0, keep_a, send_a), (half_width, keep_b, send_b)):
        right = left + half_width
        grad = mm(latent[...], dlocal[:, left:right], TN)
        grad = grad + mm(arrived_rows, back[:, left:right], TN)
        grad = grad.astype(bf16).reshape(pairs, 2, own_rows, half_width)
        keep[:, :, :half_width] = jnp.where(core == 0, grad[:, 0], grad[:, 1])
        send[:, :, :half_width] = jnp.where(core == 0, grad[:, 1], grad[:, 0])
    for store in stores:
        store.wait()


def halve_kernel(me_ref, *refs, parts):
    outs = refs[2 * len(parts) :]
    for i, (bit, (first, last), place, (left, right)) in enumerate(parts):
        keep, got = refs[2 * i], refs[2 * i + 1]
        mine = lax.rem(me_ref[0] // bit, 2)
        for out, half in ((outs[2 * place + 1], 1 - mine), (outs[2 * place], mine)):
            total = keep[:, half, :, :, first:last].astype(f32)
            total = total + got[:, half, :, :, first:last].astype(f32)
            out[:, :, :, left:right] = total.astype(bf16)


def final_kernel(keep, got, grad_w_src, grad_w_out, loss, *, scale):
    variables = grad_w_out.shape[1]
    half_width = grad_w_src.shape[1] // 2
    second = keep.shape[2] - half_width
    total = keep[0].astype(f32) + got[0].astype(f32)
    grad_w_src[:, :half_width] = total[:, :half_width] * scale
    grad_w_src[:, half_width:] = total[:, second:] * scale
    out = total[:, half_width:second]
    grad_w_out[...] = out[:, :variables] * scale
    lane = lax.broadcasted_iota(jnp.int32, out.shape, 1)
    loss[...] = jnp.sum(jnp.where(lane >= variables, out, 0.0), keepdims=True)


def latent_grad_kernel(
    rows_ref, returned, dlocal_hbm, w_src_t_hbm, out_hbm, selector, dlocal, w_src_t, out, sem
):
    shards, per_pair, width = returned.shape
    _, slots, _ = rows_ref.shape
    members = per_pair // slots
    loads = [
        pltpu.make_async_copy(w_src_t_hbm, w_src_t, sem.at[0]),
        pltpu.make_async_copy(dlocal_hbm, dlocal, sem.at[1]),
    ]
    for load in loads:
        load.start()
    fill_selector(selector, rows_ref, members)
    back = returned[...].reshape(shards * per_pair, width)
    spread = mm(selector[...].astype(bf16), back, TN)
    for load in loads:
        load.wait()
    total = (dlocal[...].astype(f32) + spread).astype(bf16)
    stores = []
    chunk = width // 4
    for i in range(4):
        part = pl.ds(i * chunk, chunk)
        out[:, part] = mm(total, w_src_t[:, part])
        stores.append(
            pltpu.make_async_copy(out.at[:, part], out_hbm.at[:, part], sem.at[2 + i])
        )
        stores[-1].start()
    for store in stores:
        store.wait()


def size_of(x):
    return math.prod(x.shape) * jnp.dtype(x.dtype).itemsize


def call(kernel, out_shape, in_specs, scratch, cost, *args, out_specs=None, limit=None):
    single = not isinstance(out_shape, (list, tuple))
    outs = [out_shape] if single else list(out_shape)
    specs = out_specs or [VMEM] * len(outs)
    used = sum(size_of(x) for x, s in zip(args, in_specs, strict=True) if s is VMEM)
    used += sum(size_of(x) for x, s in zip(outs, specs, strict=True) if s is VMEM)
    used += sum(size_of(x) for x in scratch if getattr(x, "dtype", None) in (f32, bf16))
    limit = limit or used + used // 4 + 6 * MIB
    if used > limit * 4 // 5:
        limit = 60 * MIB
    return pl.pallas_call(
        kernel,
        out_shape=out_shape,
        in_specs=in_specs,
        out_specs=specs[0] if single else specs,
        scratch_shapes=scratch,
        compiler_params=pltpu.CompilerParams(vmem_limit_bytes=limit),
        cost_estimate=pl.CostEstimate(flops=cost, bytes_accessed=used, transcendentals=0),
    )(*args)


def swap(value, bit, shards):
    return lax.ppermute(value, "space", [(i, i ^ bit) for i in range(shards)])


def per_device(
    latent,
    w_src,
    b_hidden,
    w_out,
    b_out,
    targets,
    var_weight,
    area_weight,
    edge_src,
    edge_coef,
    send_rows,
):
    mesh_rows, members, width = latent.shape
    shards = lax.axis_size("space")
    slots = send_rows.shape[2]
    variables, points = targets.shape
    points_all = points * shards
    own_rows = width // shards
    per_pair = slots * members
    rows = mesh_rows + shards * slots
    loss_columns = round_up(2 * shards, own_rows) // own_rows
    var_pad = round_up(variables + loss_columns, LANES)
    half_width = width // 2
    shape = jax.ShapeDtypeStruct
    me = lax.axis_index("space").astype(jnp.int32).reshape(1)

    latent_rows = latent.reshape(mesh_rows * members, width)
    slot_rows = jnp.swapaxes(send_rows, 1, 2)
    area_row = area_weight.reshape(1, points)
    selector = pltpu.VMEM((shards * per_pair, mesh_rows * members), f32)
    outgoing = call(
        functools.partial(pack_kernel, members=members),
        shape((shards, per_pair, width + LANES), bf16),
        [SMEM, VMEM, VMEM],
        [selector],
        1 << 24,
        slot_rows,
        latent_rows,
        area_row,
        limit=PACK * MIB,
    )
    arrived = lax.all_to_all(outgoing, "space", split_axis=0, concat_axis=0, tiled=True)

    columns = width + var_pad
    cut = half_width + var_pad
    layout = Layout(members, rows, points, var_pad, width)
    prepared, w_src_t = call(
        functools.partial(local_kernel, layout=layout, rows=rows),
        [shape(layout.shape, bf16), shape((width, width), bf16)],
        [VMEM] * 10,
        [
            pltpu.VMEM((width // LANES, mesh_rows * members, LANES), f32),
            pltpu.VMEM((var_pad, width), f32),
            pltpu.VMEM((var_pad, points), f32),
        ],
        1 << 31,
        latent_rows,
        w_src,
        edge_src.T,
        edge_coef.T,
        b_hidden.reshape(1, width),
        w_out.T,
        b_out.reshape(variables, 1),
        targets,
        var_weight.reshape(variables, 1),
        area_row,
        limit=56 * MIB,
    )

    operands = (w_src, prepared, latent_rows)
    dlocal, slot_grad, *pieces = call(
        functools.partial(
            decoder_kernel, layout=layout, points_all=points_all, variables=variables
        ),
        [
            shape((mesh_rows * members, width), bf16),
            shape((shards, per_pair, width), bf16),
            *[shape((shards // 2, own_rows, n), bf16) for n in (cut, half_width) for _ in range(2)],
        ],
        [SMEM, VMEM] + [HBM] * len(operands),
        [
            *[pltpu.VMEM(x.shape, x.dtype) for x in operands],
            pltpu.VMEM((members * points, width), bf16),
            pltpu.VMEM((members * points, width), bf16),
            pltpu.VMEM((2, points, width), f32),
            pltpu.VMEM((2, points, width), bf16),
            pltpu.VMEM((members, points, var_pad), f32),
            pltpu.VMEM((members, points, var_pad), bf16),
            pltpu.VMEM((points, var_pad), f32),
            pltpu.VMEM((points, var_pad), f32),
            pltpu.VMEM((width, var_pad), bf16),
            pltpu.VMEM((width // LANES, rows * members, LANES), f32),
            pltpu.VMEM((mesh_rows * members, width), bf16),
            pltpu.VMEM((shards, per_pair, width), bf16),
            pltpu.SemaphoreType.DMA((3,)),
        ],
        1 << 34,
        me,
        arrived,
        *operands,
        out_specs=[HBM] * 2 + [VMEM] * 4,
        limit=KEEP * MIB,
    )

    returned = lax.all_to_all(slot_grad, "space", split_axis=0, concat_axis=0, tiled=True)

    levels = [1 << i for i in reversed(range(1, shards.bit_length() - 1))]
    order_a = levels[::-1]
    order_b = order_a[1:2] + order_a[:1] + order_a[2:]
    left = [list(levels), list(levels)]
    held = [(pieces[i], swap(pieces[i + 1], 1, shards)) for i in (0, 2)]
    count = shards // 2
    for step, bits in enumerate(zip(order_a, order_b, strict=True)):
        views, parts = [], []
        for i, bit in enumerate(bits):
            place = left[i].index(bit)
            left[i].remove(bit)
            if step > 2 and i == 1:
                break
            pair = held[i]
            split = (1 << place, 2, count >> (place + 1), own_rows)
            views += [x.reshape(*split, x.shape[2]) for x in pair]
            mine = (0, cut) if i == 0 else (cut, columns)
            alone = (0, mine[1] - mine[0])
            if step < 2:
                parts.append((bit, alone, i, alone))
            elif step == 2:
                parts.append((bit, alone, 0, mine))
            else:
                parts.append((bit, (0, columns), 0, (0, columns)))
        widths = (cut, columns - cut) if step < 2 else (columns,)
        count //= 2
        outs = []
        for i, w in enumerate(widths):
            hi, _, lo = views[2 * i].shape[:3]
            outs += [shape((hi, lo, own_rows, w), bf16)] * 2
        pieces = call(
            functools.partial(halve_kernel, parts=tuple(parts)),
            outs,
            [SMEM] + [VMEM] * len(views),
            [],
            1 << 24,
            me,
            *views,
        )
        pieces = [x.reshape(count, own_rows, x.shape[3]) for x in pieces]
        held = [
            (pieces[2 * i], swap(pieces[2 * i + 1], bits[i], shards)) for i in range(len(widths))
        ]

    grad_latent = call(
        latent_grad_kernel,
        shape((mesh_rows * members, width), f32),
        [SMEM, VMEM, HBM, HBM],
        [
            selector,
            pltpu.VMEM((mesh_rows * members, width), bf16),
            pltpu.VMEM((width, width), bf16),
            pltpu.VMEM((mesh_rows * members, width), f32),
            pltpu.SemaphoreType.DMA((6,)),
        ],
        1 << 32,
        slot_rows,
        returned,
        dlocal,
        w_src_t,
        out_specs=[HBM],
        limit=LAST * MIB,
    )
    grad_w_src, grad_w_out, loss = call(
        functools.partial(final_kernel, scale=WSCALE / points_all),
        [
            shape((own_rows, width), f32),
            shape((own_rows, variables), f32),
            shape((1, 1), f32),
        ],
        [VMEM] * 2,
        [],
        1 << 24,
        *held[0],
    )
    return (
        loss.reshape(1),
        grad_latent.reshape(mesh_rows, members, width),
        grad_w_src,
        grad_w_out,
    )


def solution(mesh):
    placed = (
        P(("groups", "space"), None, None),
        P(),
        P(),
        P(),
        P(),
        P(None, ("groups", "space")),
        P(),
        P("space"),
        P("space", None),
        P("space", None),
        P("space", None, None),
    )
    return jax.shard_map(
        per_device,
        mesh=mesh,
        in_specs=placed,
        out_specs=(
            P("groups"),
            P(("groups", "space"), None, None),
            P(("groups", "space"), None),
            P(("groups", "space"), None),
        ),
        check_vma=False,
    )
```

```python
import functools
import math

import jax
import jax.numpy as jnp
from jax import lax
from jax.experimental import pallas as pl
from jax.experimental.pallas import tpu as pltpu
from jax.sharding import PartitionSpec as P

WSCALE = 2048
LANES = 128
ROWS = 16
alpha_fair = 0.95
smooth_sq = 0.01
MIB = 1 << 20
KEEP = 50
PACK = 56
LAST = 54

f32 = jnp.float32
bf16 = jnp.bfloat16
NN = (((1,), (0,)), ((), ()))
TN = (((0,), (0,)), ((), ()))
NT = (((1,), (1,)), ((), ()))
SMEM = pl.BlockSpec(memory_space=pltpu.SMEM)
VMEM = pl.BlockSpec(memory_space=pltpu.VMEM)
ANY = pl.BlockSpec(memory_space=pl.ANY)
HBM = pl.BlockSpec(memory_space=pltpu.HBM)


def spread_coef(members):
    return alpha_fair / (2.0 * members * (members - 1)) + (1.0 - alpha_fair) / (
        2.0 * members * members
    )


def mm(a, b, dims=NN):
    return lax.dot_general(a, b, dims, preferred_element_type=f32)


def round_up(value, multiple):
    return -(-value // multiple) * multiple


def split_sum(value):
    high = value.astype(bf16)
    rest = value - high.astype(f32)
    middle = rest.astype(bf16)
    return high, middle, (rest - middle.astype(f32)).astype(bf16)


def project(projected, rows, w_src):
    out = mm(rows, w_src[...])
    for c in range(projected.shape[0]):
        projected[c, : rows.shape[0], :] = out[:, c * LANES : (c + 1) * LANES]


def by_member(projected, table, members, rows_pad, first, count):
    for m in range(members):
        at = m * rows_pad + first
        for c in range(projected.shape[0]):
            block = projected[c, pl.ds(m, count, stride=members), :]
            table[at : at + count, c * LANES : (c + 1) * LANES] = block.astype(bf16)


def fill_selector(selector, rows_ref, members):
    _, slots, shards = rows_ref.shape
    lane = lax.broadcasted_iota(jnp.int32, (members, selector.shape[1]), 1)
    member = lax.broadcasted_iota(jnp.int32, (members, selector.shape[1]), 0)
    for s in range(shards):
        for b in range(slots):
            first = (s * slots + b) * members
            selector[first : first + members, :] = jnp.where(
                lane == rows_ref[0, b, s] * members + member, 1.0, 0.0
            ).astype(f32)


def pack_kernel(rows_ref, latent, area, out, selector, *, members):
    shards, per_pair, _ = out.shape
    width = latent.shape[1]
    fill_selector(selector, rows_ref, members)
    picked = mm(selector[...].astype(bf16), latent[...])
    out[:, :, :width] = picked.astype(bf16).reshape(shards, per_pair, width)
    total = jnp.sum(area[...], axis=1, keepdims=True) + jnp.zeros((per_pair, LANES), f32)
    lane = lax.broadcasted_iota(jnp.int32, (per_pair, LANES), 1)
    tail = jnp.zeros((per_pair, LANES), f32)
    for i, piece in enumerate(split_sum(total)):
        tail = jnp.where(lane == i, piece.astype(f32), tail)
    tail = tail.astype(bf16)
    for s in range(shards):
        out[s, :, width:] = tail


def strips(widths, width):
    places, strip, first = [], 0, 0
    for w in widths:
        if first + w > width:
            strip, first = strip + 1, 0
        places.append((strip, first))
        first += w
    return places, strip + 1


class Layout:
    def __init__(self, members, rows, points, var_pad, width):
        self.rows_pad = round_up(rows + 2, ROWS)
        self.out_first = members * self.rows_pad
        self.point_first = self.out_first + var_pad
        widths = [var_pad] * 6 + [round_up(self.rows_pad, LANES)]
        self.places, count = strips(widths, width)
        self.points = points
        self.edge_first = self.point_first + count * points
        self.shape = (self.edge_first + rows, width)

    def point_block(self, ref, i, columns):
        strip, first = self.places[i]
        at = self.point_first + strip * self.points
        return ref.at[pl.ds(at, self.points), pl.ds(first, columns)]


def local_kernel(
    latent,
    w_src,
    edge_src,
    edge_coef,
    b_hidden,
    w_out_t,
    b_out,
    targets,
    var_weight,
    area_weight,
    prepared,
    w_src_t,
    projected,
    wide,
    tall,
    *,
    layout,
    rows,
):
    variables, width = w_out_t.shape
    points = edge_src.shape[1]
    rows_pad = layout.rows_pad
    members = layout.out_first // rows_pad
    mesh_rows = latent.shape[0] // members
    var_pad = wide.shape[0]
    project(projected, latent[...], w_src)
    by_member(projected, prepared, members, rows_pad, 0, mesh_rows)

    row = lax.broadcasted_iota(jnp.int32, (rows_pad, points), 0)
    matrix = jnp.where((row >= rows) & (row < rows + 2), 0.5, 0.0).astype(f32)
    for k in range(edge_src.shape[0]):
        matrix = matrix + jnp.where(
            row == edge_src[k : k + 1, :], 0.5 * edge_coef[k : k + 1, :], 0.0
        )
    prepared[layout.edge_first :, :points] = matrix[:rows].astype(bf16)
    layout.point_block(prepared, 6, rows_pad)[...] = matrix.T.astype(bf16)

    high, low, _ = split_sum(b_hidden[...])
    at = lax.broadcasted_iota(jnp.int32, (rows_pad - rows, width), 0)
    bias_rows = jnp.where(
        at == 0, high.astype(f32), jnp.where(at == 1, low.astype(f32), 0.0)
    ).astype(bf16)
    for m in range(members):
        prepared[m * rows_pad + rows : (m + 1) * rows_pad, :] = bias_rows

    wide[...] = jnp.zeros_like(wide)
    wide[:variables, :] = w_out_t[...].astype(f32)
    prepared[layout.out_first : layout.point_first, :] = wide[...].astype(bf16)

    for i, value in ((0, targets[...] - b_out[...]), (3, var_weight[...] * area_weight[...])):
        tall[...] = jnp.zeros_like(tall)
        tall[:variables, :] = value
        for j, piece in enumerate(split_sum(tall[...].T)):
            layout.point_block(prepared, i + j, var_pad)[...] = piece
    w_src_t[...] = w_src[...].T


def decoder_kernel(
    me_ref,
    arrived,
    w_src_hbm,
    prepared_hbm,
    latent_hbm,
    dlocal_hbm,
    slot_grad_hbm,
    keep_a,
    send_a,
    keep_b,
    send_b,
    w_src,
    prepared,
    latent,
    hidden,
    slope,
    preact,
    dpreact,
    pred,
    dpred,
    truth,
    weighting,
    w_out_pad,
    dtable,
    dlocal,
    slot_grad,
    sem,
    *,
    layout,
    points_all,
    variables,
):
    shards, per_pair, _ = arrived.shape
    received = shards * per_pair
    own, width = latent.shape
    members, points, var_pad = pred.shape
    mesh_rows = own // members
    rows = mesh_rows + received // members
    rows_pad = layout.rows_pad
    me = me_ref[0]

    loads = [
        pltpu.make_async_copy(source, target, sem.at[i])
        for i, (source, target) in enumerate(
            ((w_src_hbm, w_src), (prepared_hbm, prepared), (latent_hbm, latent))
        )
    ]
    for load in loads:
        load.start()

    loads[0].wait()
    arrived_rows = arrived[:, :, :width].reshape(received, width)
    project(dtable, arrived_rows, w_src)
    loads[1].wait()
    by_member(dtable, prepared, members, rows_pad, mesh_rows, received // members)
    w_out_t_pad = prepared[layout.out_first : layout.point_first, :]
    w_out_pad[...] = w_out_t_pad.T
    for i, target in ((0, truth), (3, weighting)):
        target[...] = sum(
            layout.point_block(prepared, i + j, var_pad)[...].astype(f32) for j in range(3)
        )

    tail = arrived[:, :, width:].astype(f32)
    at_row = lax.broadcasted_iota(jnp.int32, tail.shape, 1)
    at_lane = lax.broadcasted_iota(jnp.int32, tail.shape, 2)
    tail = jnp.where((at_row == 0) & (at_lane < 3), tail, 0.0)
    mean_area = jnp.sum(jnp.sum(tail, axis=0), keepdims=True) / points_all

    c0 = math.sqrt(2.0 / math.pi)
    c1 = c0 * 0.044715
    quarter = width // 4

    def gather(m, slot, c):
        left, right = c * quarter, (c + 1) * quarter
        table = prepared[m * rows_pad : (m + 1) * rows_pad, left:right]
        preact[slot, :, left:right] = mm(layout.point_block(prepared, 6, rows_pad)[...], table)

    for c in range(4):
        gather(0, 0, c)

    for m in range(members):
        slot = m % 2
        first = m * points
        for c in range(4):
            left, right = c * quarter, (c + 1) * quarter
            if m + 1 < members:
                gather(m + 1, 1 - slot, c)
            for r in range(0, points, ROWS):
                y = preact[slot, r : r + ROWS, left:right]
                y2 = y * y
                t = jnp.tanh(y * (2.0 * c0 + (8.0 * c1) * y2))
                p = 1.0 + t
                gelu = y * p
                hidden[first + r : first + r + ROWS, left:right] = gelu.astype(bf16)
                bend = (gelu * (1.0 - t)) * (2.0 * c0 + (24.0 * c1) * y2)
                slope[first + r : first + r + ROWS, left:right] = (p + bend).astype(bf16)
        pred[m] = mm(hidden[first : first + points, :], w_out_pad[...])

    spread = spread_coef(members)
    inverse_mean = 1.0 / mean_area
    loss_sum = jnp.zeros((ROWS, LANES), f32)
    for left in range(0, var_pad, LANES):

        def score(block, loss_sum, left=left):
            at = pl.ds(pl.multiple_of(block * ROWS, ROWS), ROWS)
            p = [pred[m, at, left : left + LANES] for m in range(members)]
            true = truth[at, left : left + LANES]
            weight = weighting[at, left : left + LANES]
            fit = jnp.zeros((ROWS, LANES), f32)
            grads = []
            for m in range(members):
                d = p[m] - true
                q = d * d + smooth_sq
                r = lax.rsqrt(q)
                fit = fit + q * r
                grads.append(d * r)
            pairs = jnp.zeros((ROWS, LANES), f32)
            apart = [jnp.zeros((ROWS, LANES), f32) for _ in range(members)]
            for j in range(members):
                for k in range(j + 1, members):
                    d = p[j] - p[k]
                    q = d * d + smooth_sq
                    r = lax.rsqrt(q)
                    pairs = pairs + q * r
                    s = d * r
                    apart[j] = apart[j] + s
                    apart[k] = apart[k] - s
            scaled = weight * (inverse_mean * (1.0 / members))
            for m in range(members):
                gradient = grads[m] - (2.0 * spread * members) * apart[m]
                dpred[m, at, left : left + LANES] = (gradient * scaled).astype(bf16)
            return loss_sum + weight * (fit * (1.0 / members) - (2.0 * spread) * pairs)

        loss_sum = lax.fori_loop(0, points // ROWS, score, loss_sum, unroll=2)
    loss = jnp.sum(loss_sum, keepdims=True) * (inverse_mean / points_all)

    edge_back = prepared[layout.edge_first :, :points]
    preact[0] = mm(dpred[0], w_out_t_pad)
    for m in range(members + 1):
        if m + 1 < members:
            preact[(m + 1) % 2] = mm(dpred[m + 1], w_out_t_pad)
        if m < members:
            for r in range(0, points, ROWS):
                at = m * points + r
                grad = preact[m % 2, r : r + ROWS, :] * slope[at : at + ROWS, :].astype(f32)
                dpreact[m % 2, r : r + ROWS, :] = grad.astype(bf16)
        if m >= 1:
            grad = mm(edge_back, dpreact[(m - 1) % 2])
            for c in range(width // LANES):
                dtable[c, pl.ds(m - 1, rows, stride=members), :] = grad[
                    :, c * LANES : (c + 1) * LANES
                ]

    for c in range(width // LANES):
        left, right = c * LANES, (c + 1) * LANES
        dlocal[:, left:right] = dtable[c, :own, :].astype(bf16)
        slot_grad[:, :, left:right] = (
            dtable[c, own:, :].astype(bf16).reshape(shards, per_pair, LANES)
        )
    stores = [
        pltpu.make_async_copy(slot_grad, slot_grad_hbm, sem.at[0]),
        pltpu.make_async_copy(dlocal, dlocal_hbm, sem.at[1]),
    ]
    for store in stores:
        store.start()

    half_width = width // 2
    pairs, own_rows, _ = keep_a.shape
    core = lax.rem(me, 2)
    grad = mm(dpred[...].reshape(members * points, var_pad), hidden[...], TN).T
    row = lax.broadcasted_iota(jnp.int32, grad.shape, 0)
    lane = lax.broadcasted_iota(jnp.int32, grad.shape, 1)
    row = row & (own_rows - 1)
    grad = jnp.where(lane < variables, grad, 0.0)
    for i, piece in enumerate(split_sum(loss)[:2]):
        place = me * 2 + i
        here = (row == lax.rem(place, own_rows)) & (lane == variables + place // own_rows)
        grad = jnp.where(here, piece.astype(f32), grad)
    grad = grad.astype(bf16).reshape(pairs, 2, own_rows, var_pad)
    keep_a[:, :, half_width:] = jnp.where(core == 0, grad[:, 0], grad[:, 1])
    send_a[:, :, half_width:] = jnp.where(core == 0, grad[:, 1], grad[:, 0])
    loads[2].wait()
    back = slot_grad[...].reshape(received, width)
    for left, keep, send in ((0, keep_a, send_a), (half_width, keep_b, send_b)):
        right = left + half_width
        grad = mm(latent[...], dlocal[:, left:right], TN)
        grad = grad + mm(arrived_rows, back[:, left:right], TN)
        grad = grad.astype(bf16).reshape(pairs, 2, own_rows, half_width)
        keep[:, :, :half_width] = jnp.where(core == 0, grad[:, 0], grad[:, 1])
        send[:, :, :half_width] = jnp.where(core == 0, grad[:, 1], grad[:, 0])
    for store in stores:
        store.wait()


def halve_kernel(me_ref, *refs, parts):
    outs = refs[2 * len(parts) :]
    for i, (bit, (first, last), place, (left, right)) in enumerate(parts):
        keep, got = refs[2 * i], refs[2 * i + 1]
        mine = lax.rem(me_ref[0] // bit, 2)
        for out, half in ((outs[2 * place + 1], 1 - mine), (outs[2 * place], mine)):
            total = keep[:, half, :, :, first:last].astype(f32)
            total = total + got[:, half, :, :, first:last].astype(f32)
            out[:, :, :, left:right] = total.astype(bf16)


def final_kernel(keep, got, grad_w_src, grad_w_out, loss, *, scale):
    variables = grad_w_out.shape[1]
    half_width = grad_w_src.shape[1] // 2
    second = keep.shape[2] - half_width
    total = keep[0].astype(f32) + got[0].astype(f32)
    grad_w_src[:, :half_width] = total[:, :half_width] * scale
    grad_w_src[:, half_width:] = total[:, second:] * scale
    out = total[:, half_width:second]
    grad_w_out[...] = out[:, :variables] * scale
    lane = lax.broadcasted_iota(jnp.int32, out.shape, 1)
    loss[...] = jnp.sum(jnp.where(lane >= variables, out, 0.0), keepdims=True)


def latent_grad_kernel(
    rows_ref, returned, dlocal_hbm, w_src_t_hbm, out_hbm, selector, dlocal, w_src_t, out, sem
):
    shards, per_pair, width = returned.shape
    _, slots, _ = rows_ref.shape
    members = per_pair // slots
    loads = [
        pltpu.make_async_copy(w_src_t_hbm, w_src_t, sem.at[0]),
        pltpu.make_async_copy(dlocal_hbm, dlocal, sem.at[1]),
    ]
    for load in loads:
        load.start()
    fill_selector(selector, rows_ref, members)
    back = returned[...].reshape(shards * per_pair, width)
    spread = mm(selector[...].astype(bf16), back, TN)
    for load in loads:
        load.wait()
    total = (dlocal[...].astype(f32) + spread).astype(bf16)
    stores = []
    chunk = width // 4
    for i in range(4):
        part = pl.ds(i * chunk, chunk)
        out[:, part] = mm(total, w_src_t[:, part])
        stores.append(
            pltpu.make_async_copy(out.at[:, part], out_hbm.at[:, part], sem.at[2 + i])
        )
        stores[-1].start()
    for store in stores:
        store.wait()


def size_of(x):
    return math.prod(x.shape) * jnp.dtype(x.dtype).itemsize


def call(kernel, out_shape, in_specs, scratch, cost, *args, out_specs=None, limit=None):
    single = not isinstance(out_shape, (list, tuple))
    outs = [out_shape] if single else list(out_shape)
    specs = out_specs or [VMEM] * len(outs)
    used = sum(size_of(x) for x, s in zip(args, in_specs, strict=True) if s is VMEM)
    used += sum(size_of(x) for x, s in zip(outs, specs, strict=True) if s is VMEM)
    used += sum(size_of(x) for x in scratch if getattr(x, "dtype", None) in (f32, bf16))
    limit = limit or used + used // 4 + 6 * MIB
    if used > limit * 4 // 5:
        limit = 60 * MIB
    return pl.pallas_call(
        kernel,
        out_shape=out_shape,
        in_specs=in_specs,
        out_specs=specs[0] if single else specs,
        scratch_shapes=scratch,
        compiler_params=pltpu.CompilerParams(vmem_limit_bytes=limit),
        cost_estimate=pl.CostEstimate(flops=cost, bytes_accessed=used, transcendentals=0),
    )(*args)


def swap(value, bit, shards):
    return lax.ppermute(value, "space", [(i, i ^ bit) for i in range(shards)])


def per_device(
    latent,
    w_src,
    b_hidden,
    w_out,
    b_out,
    targets,
    var_weight,
    area_weight,
    edge_src,
    edge_coef,
    send_rows,
):
    mesh_rows, members, width = latent.shape
    shards = lax.axis_size("space")
    slots = send_rows.shape[2]
    variables, points = targets.shape
    points_all = points * shards
    own_rows = width // shards
    per_pair = slots * members
    rows = mesh_rows + shards * slots
    loss_columns = round_up(2 * shards, own_rows) // own_rows
    var_pad = round_up(variables + loss_columns, LANES)
    half_width = width // 2
    shape = jax.ShapeDtypeStruct
    me = lax.axis_index("space").astype(jnp.int32).reshape(1)

    latent_rows = latent.reshape(mesh_rows * members, width)
    slot_rows = jnp.swapaxes(send_rows, 1, 2)
    area_row = area_weight.reshape(1, points)
    selector = pltpu.VMEM((shards * per_pair, mesh_rows * members), f32)
    outgoing = call(
        functools.partial(pack_kernel, members=members),
        shape((shards, per_pair, width + LANES), bf16),
        [SMEM, VMEM, VMEM],
        [selector],
        1 << 24,
        slot_rows,
        latent_rows,
        area_row,
        limit=PACK * MIB,
    )
    arrived = lax.all_to_all(outgoing, "space", split_axis=0, concat_axis=0, tiled=True)

    columns = width + var_pad
    cut = half_width + var_pad
    layout = Layout(members, rows, points, var_pad, width)
    prepared, w_src_t = call(
        functools.partial(local_kernel, layout=layout, rows=rows),
        [shape(layout.shape, bf16), shape((width, width), bf16)],
        [VMEM] * 10,
        [
            pltpu.VMEM((width // LANES, mesh_rows * members, LANES), f32),
            pltpu.VMEM((var_pad, width), f32),
            pltpu.VMEM((var_pad, points), f32),
        ],
        1 << 31,
        latent_rows,
        w_src,
        edge_src.T,
        edge_coef.T,
        b_hidden.reshape(1, width),
        w_out.T,
        b_out.reshape(variables, 1),
        targets,
        var_weight.reshape(variables, 1),
        area_row,
        limit=56 * MIB,
    )

    operands = (w_src, prepared, latent_rows)
    dlocal, slot_grad, *pieces = call(
        functools.partial(
            decoder_kernel, layout=layout, points_all=points_all, variables=variables
        ),
        [
            shape((mesh_rows * members, width), bf16),
            shape((shards, per_pair, width), bf16),
            *[shape((shards // 2, own_rows, n), bf16) for n in (cut, half_width) for _ in range(2)],
        ],
        [SMEM, VMEM] + [HBM] * len(operands),
        [
            *[pltpu.VMEM(x.shape, x.dtype) for x in operands],
            pltpu.VMEM((members * points, width), bf16),
            pltpu.VMEM((members * points, width), bf16),
            pltpu.VMEM((2, points, width), f32),
            pltpu.VMEM((2, points, width), bf16),
            pltpu.VMEM((members, points, var_pad), f32),
            pltpu.VMEM((members, points, var_pad), bf16),
            pltpu.VMEM((points, var_pad), f32),
            pltpu.VMEM((points, var_pad), f32),
            pltpu.VMEM((width, var_pad), bf16),
            pltpu.VMEM((width // LANES, rows * members, LANES), f32),
            pltpu.VMEM((mesh_rows * members, width), bf16),
            pltpu.VMEM((shards, per_pair, width), bf16),
            pltpu.SemaphoreType.DMA((3,)),
        ],
        1 << 34,
        me,
        arrived,
        *operands,
        out_specs=[HBM] * 2 + [VMEM] * 4,
        limit=KEEP * MIB,
    )

    returned = lax.all_to_all(slot_grad, "space", split_axis=0, concat_axis=0, tiled=True)

    levels = [1 << i for i in reversed(range(1, shards.bit_length() - 1))]
    order_a = levels[::-1]
    order_b = order_a[1:2] + order_a[:1] + order_a[2:]
    left = [list(levels), list(levels)]
    held = [(pieces[i], swap(pieces[i + 1], 1, shards)) for i in (0, 2)]
    count = shards // 2
    for step, bits in enumerate(zip(order_a, order_b, strict=True)):
        views, parts = [], []
        for i, bit in enumerate(bits):
            place = left[i].index(bit)
            left[i].remove(bit)
            if step > 2 and i == 1:
                break
            pair = held[i]
            split = (1 << place, 2, count >> (place + 1), own_rows)
            views += [x.reshape(*split, x.shape[2]) for x in pair]
            mine = (0, cut) if i == 0 else (cut, columns)
            alone = (0, mine[1] - mine[0])
            if step < 2:
                parts.append((bit, alone, i, alone))
            elif step == 2:
                parts.append((bit, alone, 0, mine))
            else:
                parts.append((bit, (0, columns), 0, (0, columns)))
        widths = (cut, columns - cut) if step < 2 else (columns,)
        count //= 2
        outs = []
        for i, w in enumerate(widths):
            hi, _, lo = views[2 * i].shape[:3]
            outs += [shape((hi, lo, own_rows, w), bf16)] * 2
        pieces = call(
            functools.partial(halve_kernel, parts=tuple(parts)),
            outs,
            [SMEM] + [VMEM] * len(views),
            [],
            1 << 24,
            me,
            *views,
        )
        pieces = [x.reshape(count, own_rows, x.shape[3]) for x in pieces]
        held = [
            (pieces[2 * i], swap(pieces[2 * i + 1], bits[i], shards)) for i in range(len(widths))
        ]

    grad_latent = call(
        latent_grad_kernel,
        shape((mesh_rows * members, width), f32),
        [SMEM, VMEM, HBM, HBM],
        [
            selector,
            pltpu.VMEM((mesh_rows * members, width), bf16),
            pltpu.VMEM((width, width), bf16),
            pltpu.VMEM((mesh_rows * members, width), f32),
            pltpu.SemaphoreType.DMA((6,)),
        ],
        1 << 32,
        slot_rows,
        returned,
        dlocal,
        w_src_t,
        out_specs=[HBM],
        limit=LAST * MIB,
    )
    grad_w_src, grad_w_out, loss = call(
        functools.partial(final_kernel, scale=WSCALE / points_all),
        [
            shape((own_rows, width), f32),
            shape((own_rows, variables), f32),
            shape((1, 1), f32),
        ],
        [VMEM] * 2,
        [],
        1 << 24,
        *held[0],
    )
    return (
        loss.reshape(1),
        grad_latent.reshape(mesh_rows, members, width),
        grad_w_src,
        grad_w_out,
    )


def solution(mesh):
    placed = (
        P(("groups", "space"), None, None),
        P(),
        P(),
        P(),
        P(),
        P(None, ("groups", "space")),
        P(),
        P("space"),
        P("space", None),
        P("space", None),
        P("space", None, None),
    )
    return jax.shard_map(
        per_device,
        mesh=mesh,
        in_specs=placed,
        out_specs=(
            P("groups"),
            P(("groups", "space"), None, None),
            P(("groups", "space"), None),
            P(("groups", "space"), None),
        ),
        check_vma=False,
    )
```
